256 devices in a mesh: eig: 64 (over y_hi, x, z), site: 4 (over y_lo, core).
Axes of the slice: x: 4, y: 4 (y_hi: 2, y_lo: 2; y = y_hi * 2 + y_lo), z: 8, core: 2. Of those that a mesh axis runs over, the one named last changes fastest.
Arguments:
- vectors: bfloat16 [2048, 102400], P('eig', 'site'), may hold values from -6 to 6
- rotation: bfloat16 [2048, 2048], P(('eig', 'site')), may hold values from -0.1875 to 0.1875
- locked: int32 [16], replicated, may hold values from 0 to 128
Outputs:
- rotated: bfloat16 [2048, 102400], P('eig', 'site')
The draws below stay inside these ranges and needn't reach their ends.
All inputs are finite; a program needn't handle non-finite values.
Results may differ from the reference program's by a relative error of at most 0.001.
Values may be sent and summed in bfloat16 or wider, within the bound.
No kernel may reach another device: no remote copies, remote signals or barrier semaphores. Data moves between devices by JAX's collectives and lax.ppermute only.
A program may use at most 128 MiB of HBM per device.

```python
import jax
import jax.numpy as jnp
from jax import lax

NVEC = 2048
BLOCK = 128
COEF = 800
NBLK = 16
NSITE = 128


def plant(array, stream_key, low, top_value):
    place = [jax.random.randint(jax.random.fold_in(stream_key, axis), (), 0, length) for axis, length in enumerate(array.shape)]
    main_axis = array.shape.index(max(array.shape))
    beside = place[:main_axis] + [(place[main_axis] + 1) % array.shape[main_axis]] + place[main_axis + 1:]
    return array.at[tuple(place)].set(low).at[tuple(beside)].set(top_value)


def steps_of(rng, extent, pieces, least, largest):
    def one(axis_at, blocks):
        draws = jax.random.uniform(jax.random.fold_in(jax.random.fold_in(rng, 6), axis_at), (blocks,), jnp.float32, least / len(pieces), largest / len(pieces))
        return jnp.repeat(jnp.exp(draws), extent[axis_at] // blocks).reshape((-1,) + (1,) * (len(extent) - axis_at - 1))

    level = one(*pieces[0])
    for cut in pieces[1:]:
        level = level * one(*cut)
    return level


def normal_values(stream_key, shape, deviation, most, split=(), kind=jnp.bfloat16):
    entries = jax.random.normal(stream_key, shape, jnp.float32) * deviation
    if len(split) > 0:
        entries = steps_of(stream_key, shape, split, -0.22, 0.18) * entries
    return jnp.clip(entries, min=-most, max=most).astype(kind)


def setup_inputs(seed: int = 0) -> dict:
    keys = jax.random.split(jax.random.key(seed), 4)
    return {
        "vectors": normal_values(keys[0], (NVEC, NSITE * COEF), 1.0, 6.0, ((0, 64), (1, 4))),
        "rotation": normal_values(keys[1], (NVEC, NVEC), (NVEC // 2) ** -0.5, 0.1875, ((0, 256),)),
        "locked": plant(jax.random.randint(keys[2], (NBLK,), 0, BLOCK + 1), jax.random.fold_in(keys[2], 1), 0, BLOCK).astype(jnp.int32),
    }


def effective_rows(panel, start, locked, block):
    count = panel.shape[0]
    width = panel.shape[1]
    rows = start + jnp.arange(count, dtype=jnp.int32)[:, None]
    cols = jnp.arange(width, dtype=jnp.int32)
    col_block = cols // block
    blocks = jnp.arange(locked.shape[0], dtype=jnp.int32)
    lock_cols = jnp.sum(jnp.where(col_block[:, None] == blocks[None, :], locked[None, :], 0), axis=1).astype(jnp.int32)
    is_locked = (cols % block) < lock_cols
    identity = jnp.where(rows == cols[None, :], 1.0, 0.0).astype(panel.dtype)
    lower = jnp.where(rows // block >= col_block[None, :], panel, jnp.zeros_like(panel))
    return jnp.where(is_locked[None, :], identity, lower)


def reference(vectors, rotation, locked):
    effective = effective_rows(rotation, jnp.int32(0), locked, BLOCK)
    product = lax.dot_general(effective, vectors, (((0,), (0,)), ((), ())), preferred_element_type=jnp.float32)
    return product.astype(jnp.bfloat16)
```

```python
import jax
import jax.numpy as jnp
from jax import lax
from jax.experimental import pallas as pl
from jax.experimental.pallas import tpu as pltpu
from jax.sharding import Mesh, PartitionSpec as P

AXES = ("yh", "x", "z", "yl", "c")
EIG = ("yh", "x", "z")
SITE = ("yl", "c")
PEERS = 64
ROWS = 32
TILES = 3
CHUNK = 104
KEEP = 1152
WIDTH = 512
HALF = 1024
F32 = jnp.float32
BF16 = jnp.bfloat16


def lane_group():
    return lax.broadcasted_iota(jnp.int32, (8, 128), 1) // 16


def low_half():
    return lax.broadcasted_iota(jnp.int32, (8, 128), 0) < 4


def regroup(tile):
    low = low_half()
    groups = []
    for k in range(4):
        straight = tile[8 * k : 8 * k + 8]
        turned = pltpu.roll(straight, 4, 0)
        groups.append(jnp.where(low, straight, turned))
        groups.append(jnp.where(low, turned, straight))
    return groups


def gather_lanes(groups, place):
    lanes = lane_group()
    total = jnp.zeros((8, 128), F32)
    for h in range(8):
        total = jnp.where(lanes == h, pltpu.roll(groups[h], (16 * (h - place)) % 128, 1), total)
    return total


def pack_kernel(main_ref, left_ref, out_ref):
    def reorder(tile):
        tile = tile.astype(F32)
        return jnp.concatenate([tile[0:8], tile[16:24], tile[8:16], tile[24:32]], axis=0)

    for part in range(2):
        groups = regroup(reorder(left_ref[:, 128 * part : 128 * part + 128]))
        for m in range(8):
            peer = 8 * part + m
            for t in range(TILES):
                column = (TILES * peer + t) * 128
                out_ref[peer, 32 * t : 32 * t + 32, :] = reorder(main_ref[:, column : column + 128]).astype(BF16)
            out_ref[peer, 96:104, :] = gather_lanes(groups, m).astype(BF16)


def pack(vectors):
    return pl.pallas_call(
        pack_kernel,
        grid=(4,),
        in_specs=[
            pl.BlockSpec((ROWS, 6144), lambda t: (0, t)),
            pl.BlockSpec((ROWS, 256), lambda t: (0, 96 + t)),
        ],
        out_specs=pl.BlockSpec((16, CHUNK, 128), lambda t: (t, 0, 0)),
        out_shape=jax.ShapeDtypeStruct((PEERS, CHUNK, 128), BF16),
    )(vectors, vectors)


def unpack_kernel(in_ref, main_ref, left_ref):
    lanes, low = lane_group(), low_half()
    lefts = []
    for m in range(8):
        for t in range(TILES):
            column = (TILES * m + t) * 128
            main_ref[:, column : column + 128] = in_ref[m, 32 * t : 32 * t + 32, :]
        lefts.append(in_ref[m, 96:104, :].astype(F32))
    pieces = []
    for k in range(4):
        total = jnp.zeros((8, 128), F32)
        for m in range(8):
            piece = jnp.where(
                low,
                pltpu.roll(lefts[m], (16 * (m - 2 * k)) % 128, 1),
                pltpu.roll(lefts[m], (16 * (m - 2 * k - 1)) % 128, 1),
            )
            total = jnp.where(lanes == m, piece, total)
        pieces.append(total)
    left_ref[...] = jnp.concatenate(pieces, axis=0).astype(BF16)


def unpack_body(in_ref, out_ref):
    for t in range(8):
        unpack_kernel(
            in_ref.at[pl.ds(8 * t, 8)],
            out_ref.at[:, pl.ds(3072 * t, 3072)],
            out_ref.at[:, pl.ds(24576 + 128 * t, 128)],
        )


def unpack(received):
    return pl.pallas_call(
        unpack_body,
        out_shape=jax.ShapeDtypeStruct((ROWS, 25600), BF16),
        compiler_params=pltpu.CompilerParams(vmem_limit_bytes=32 * 1024 * 1024),
    )(received)


def place_kernel(place_ref, *refs):
    panels, out_ref = refs[:12], refs[12]
    core, yh, x, z = (place_ref[i] for i in range(4))
    for side in range(2):
        half = core if side == 0 else 1 - core
        for first in range(2):
            for dx in range(4):
                group = (yh ^ first) * 4 + (x ^ dx)
                for step in range(8):
                    source, at = (panels[6 * side + first], dx) if step < 4 else (panels[6 * side + 2 + dx], first)
                    row = 16 * (step % 4)
                    out_ref[half, group * 8 + (z ^ step)] = source[at, row : row + 16, :]
    for group in range(8):
        slot, column = (group, 256 * group + 128) if group < 4 else (7 - group, 256 * (8 - group) + 128 * (2 * group - 8))
        for half in range(2):
            out_ref[half, 8 * slot : 8 * slot + 4, :, column : column + 128] = jnp.zeros((4, 16, 128), BF16)


def place_panels(place, panels):
    vmem = pl.BlockSpec(memory_space=pltpu.VMEM)
    return pl.pallas_call(
        place_kernel,
        in_specs=[pl.BlockSpec(memory_space=pltpu.SMEM)] + [vmem] * 12,
        out_specs=vmem,
        out_shape=jax.ShapeDtypeStruct((2, PEERS, 16, KEEP), BF16),
        compiler_params=pltpu.CompilerParams(vmem_limit_bytes=16 * 1024 * 1024),
    )(place, *panels)


def rotate_kernel(locked_ref, in_ref, source_ref, out_ref, held, matrix_ref, sems):
    copies = []
    for index, width in enumerate((256, 256, 256, 256, 128)):
        columns = (slice(None), slice(None), slice(None), pl.ds(256 * index, width))
        copies.append(pltpu.make_async_copy(source_ref.at[columns], matrix_ref.at[columns], sems.at[index]))
        copies[-1].start()
    low64 = lax.broadcasted_iota(jnp.int32, (64, 128), 0) % 8 < 4
    for group in range(8):
        rows = slice(128 * group, 128 * group + 128)
        left = in_ref[:, group, 96:104, :].astype(F32).reshape(64, 128)
        for half in range(2):
            parts = []
            for k in (2 * half, 2 * half + 1):
                a = pltpu.roll(left, (-32 * k) % 128, 1)
                b = pltpu.roll(left, (-32 * k - 16) % 128, 1)
                parts.append(jnp.where(low64, a, b).reshape(8, 8, 128))
            held[half, rows, 384:512] = jnp.stack(parts, axis=1).reshape(128, 128).astype(BF16)
            for t in range(TILES):
                part = in_ref[:, group, 32 * t + 16 * half : 32 * t + 16 * half + 16, :]
                held[half, rows, 128 * t : 128 * t + 128] = part.reshape(128, 128)

    def product(lhs, rhs):
        return lax.dot_general(lhs, rhs, (((0,), (0,)), ((), ())), preferred_element_type=F32)

    def natural(first, second):
        pair = [v.astype(F32).reshape(8, 2, 1, 8, 128) for v in (first, second)]
        return jnp.concatenate(pair, axis=2).reshape(256, 128)

    for block in range(8):
        for copy in copies[block : block + 1]:
            copy.wait()
        total = None
        for half in range(2):

            def panel(group, column, width, groups=1):
                return matrix_ref[half, 8 * group : 8 * (group + groups), :, column : column + width].reshape(128 * groups, width)

            terms = []
            if block < 4:
                terms.append((panel(block, 256 * block, 256, 8 - block), held[half, 128 * block : HALF, :]))
            for peer in range(block, 8) if block >= 4 else ():
                at = 256 * (8 - peer) + 128 * (2 * block - 9)
                if block == 4:
                    lhs = jnp.concatenate([panel(peer, 1024, 128), panel(7 - peer, at + 128, 128)], axis=1)
                else:
                    lhs = panel(7 - peer, at, 256)
                terms.append((lhs, held[half, 128 * peer : 128 * peer + 128, :]))
            for lhs, rhs in terms:
                term = product(lhs, rhs)
                total = term if total is None else total + term
        rows = lax.broadcasted_iota(jnp.int32, (256, 1), 0)
        limit = jnp.where(rows < 128, locked_ref[2 * block], locked_ref[2 * block + 1])
        kept = rows % 128 < limit
        peers = slice(8 * block, 8 * block + 8)
        for t in range(TILES):
            mine = natural(*(in_ref[:, block, 32 * t + at : 32 * t + at + 16, :] for at in (0, 16)))
            result = jnp.where(kept, mine, total[:, 128 * t : 128 * t + 128]).astype(BF16)
            out_ref[peers, 32 * t : 32 * t + 32, :] = result.reshape(8, 32, 128)
        mine = natural(held[0, 128 * block : 128 * block + 128, 384:512], held[1, 128 * block : 128 * block + 128, 384:512])
        result = jnp.where(kept, mine, total[:, 384:512]).astype(BF16).astype(F32)
        for m in range(8):
            groups = regroup(result[32 * m : 32 * m + 32])
            out_ref[8 * block + m, 96:104, :] = gather_lanes(groups, 0).astype(BF16)


def rotate(locked, received, matrix):
    vmem = pl.BlockSpec(memory_space=pltpu.VMEM)
    return pl.pallas_call(
        rotate_kernel,
        in_specs=[pl.BlockSpec(memory_space=pltpu.SMEM), vmem, pl.BlockSpec(memory_space=pl.ANY)],
        out_specs=vmem,
        out_shape=jax.ShapeDtypeStruct((PEERS, CHUNK, 128), BF16),
        scratch_shapes=[
            pltpu.VMEM((2, HALF, WIDTH), BF16),
            pltpu.VMEM((2, PEERS, 16, KEEP), BF16),
            pltpu.SemaphoreType.DMA((5,)),
        ],
        compiler_params=pltpu.CompilerParams(vmem_limit_bytes=56 * 1024 * 1024),
    )(locked, received, matrix)


def exchange(value, axis, size, mask):
    return lax.ppermute(value, axis, [(i, i ^ mask) for i in range(size)])


def gather_near(rotation):
    rows = rotation[None]
    rows = jnp.concatenate([rows] + [exchange(rows, "z", 8, step) for step in (1, 2, 3)])
    late = [i for i in range(PEERS) if i >= 32]
    spare = rows[:, :, KEEP:]
    guests = [lax.ppermute(spare, EIG, [(i, (7 - i // 8) * 8 + (i % 8 ^ far)) for i in late]) for far in (0, 4)]
    return rows[:, :, :KEEP], exchange(rows[:, :, :KEEP], "z", 8, 4), *guests


def gather_panels(near, far, *guests):
    eig, yl = lax.axis_index(EIG), lax.axis_index("yl")
    group = eig // 8
    rows = jnp.concatenate([near, far])
    place = 256 * (group + 1)
    guest = jnp.concatenate([jnp.concatenate(guests), jnp.zeros((8, 8, KEEP), BF16)], axis=2)
    guest = lax.dynamic_update_slice(jnp.zeros((8, 8, 4096), BF16), guest, (0, 0, place))[:, :, :KEEP]
    cols = lax.broadcasted_iota(jnp.int32, (1, 1, KEEP), 2)
    rows = jnp.where((group >= 4) | (cols < place), rows, guest)
    other = exchange(rows, "yl", 2, 1)
    rows = jnp.where(yl == 0, jnp.stack([rows, other], axis=1), jnp.stack([other, rows], axis=1))

    a, b = rows[:4].reshape(1, 64, KEEP), rows[4:].reshape(1, 64, KEEP)
    b = jnp.concatenate([b, exchange(b, "yh", 2, 1)])
    a = jnp.concatenate([a] + [exchange(a, "x", 4, dx) for dx in (1, 2, 3)])
    far_a = exchange(a, "yh", 2, 1)
    far_b = [exchange(b, "x", 4, dx) for dx in (1, 2, 3)]
    a, b, far_a = lax.optimization_barrier((a, b, far_a))
    own = [a, far_a, b] + far_b
    return own + [exchange(panel, "c", 2, 1) for panel in own]


def body(vectors, rotation, locked):
    packed = pack(vectors).reshape(8, 8, CHUNK, 128)
    halfway = lax.all_to_all(packed, ("yh", "x"), split_axis=0, concat_axis=0, tiled=True)
    near, far, *guests = gather_near(rotation)
    halfway, near, far = lax.optimization_barrier((halfway, near, far))
    place = jnp.stack([lax.axis_index(name) for name in ("c", "yh", "x", "z")]).astype(jnp.int32)
    matrix = place_panels(place, gather_panels(near, far, *guests))
    received = lax.all_to_all(halfway.transpose(1, 0, 2, 3), "z", split_axis=0, concat_axis=0, tiled=True)
    back = lax.all_to_all(rotate(locked, received, matrix), EIG, split_axis=0, concat_axis=0, tiled=True)
    return unpack(back)


def solution(mesh):
    fine = Mesh(mesh.devices.reshape(2, 4, 8, 2, 2), AXES)
    in_specs = (P(EIG, SITE), P(EIG + SITE, None), P())
    return jax.shard_map(body, mesh=fine, in_specs=in_specs, out_specs=P(EIG, SITE), check_vma=False)
```

```python
import functools

import jax
import jax.numpy as jnp
from jax import lax
from jax.experimental import pallas as pl
from jax.experimental.pallas import tpu as pltpu
from jax.sharding import Mesh, PartitionSpec as P

AXES = ("yh", "x", "zh", "zl", "yl", "c")
Z = ("zh", "zl")
EIG = ("yh", "x", "zh", "zl")
SITE = ("yl", "c")
PEERS = 64
ROWS = 32
TILES = 3
CHUNK = 104
KEEP = 1152
WIDTH = 512
F32 = jnp.float32
BF16 = jnp.bfloat16


def seat(z):
    return z % 4 * 2 + z // 4


def place_of(peer):
    yh, x, z = peer // 32, peer // 8 % 4, peer % 8
    return ((x * 4 + z % 4) * 2 + yh) * 2 + z // 4


def lane_group():
    return lax.broadcasted_iota(jnp.int32, (8, 128), 1) // 16


def low_half():
    return lax.broadcasted_iota(jnp.int32, (8, 128), 0) < 4


def regroup(tile):
    low = low_half()
    groups = []
    for k in range(4):
        straight = tile[8 * k : 8 * k + 8]
        turned = pltpu.roll(straight, 4, 0)
        groups.append(jnp.where(low, straight, turned))
        groups.append(jnp.where(low, turned, straight))
    return groups


def gather_lanes(groups, place):
    lanes = lane_group()
    total = jnp.zeros((8, 128), F32)
    for h in range(8):
        total = jnp.where(lanes == h, pltpu.roll(groups[h], (16 * (h - place)) % 128, 1), total)
    return total


def pack_kernel(in_ref, out_ref):
    for group in range(8):
        column = 24576 + 128 * group
        groups = regroup(in_ref[:, column : column + 128].astype(F32))
        for z in range(8):
            for t in range(TILES):
                column = (TILES * (8 * group + z) + t) * 128
                out_ref[group, seat(z), 32 * t : 32 * t + 32, :] = in_ref[:, column : column + 128]
            out_ref[group, seat(z), 96:104, :] = gather_lanes(groups, z).astype(BF16)


def pack(vectors):
    return pl.pallas_call(
        pack_kernel,
        out_shape=jax.ShapeDtypeStruct((8, 8, CHUNK, 128), BF16),
        compiler_params=pltpu.CompilerParams(vmem_limit_bytes=16 * 1024 * 1024),
    )(vectors)


def unpack_kernel(in_ref, out_ref):
    lanes, low = lane_group(), low_half()
    for group in range(8):
        lefts = []
        for z in range(8):
            seat_of = place_of(8 * group + z)
            for t in range(TILES):
                column = (TILES * (8 * group + z) + t) * 128
                out_ref[:, column : column + 128] = in_ref[seat_of, 32 * t : 32 * t + 32, :]
            lefts.append(in_ref[seat_of, 96:104, :].astype(F32))
        pieces = []
        for k in range(4):
            total = jnp.zeros((8, 128), F32)
            for z in range(8):
                first = pltpu.roll(lefts[z], (16 * (z - 2 * k)) % 128, 1)
                second = pltpu.roll(lefts[z], (16 * (z - 2 * k - 1)) % 128, 1)
                total = jnp.where(lanes == z, jnp.where(low, first, second), total)
            pieces.append(total)
        column = 24576 + 128 * group
        out_ref[:, column : column + 128] = jnp.concatenate(pieces, axis=0).astype(BF16)


def unpack(received):
    return pl.pallas_call(
        unpack_kernel,
        out_shape=jax.ShapeDtypeStruct((ROWS, 25600), BF16),
        compiler_params=pltpu.CompilerParams(vmem_limit_bytes=16 * 1024 * 1024),
    )(received)


def place_kernel(place_ref, *refs):
    panels, out_ref = refs[:12], refs[12]
    core, yh, x, z = (place_ref[i] for i in range(4))

    def fill(first_side):
        for first in range(2):
            for dx in range(4):
                group = (yh ^ first) * 4 + (x ^ dx)
                for step in range(8):
                    which, at = (first, dx) if step < 4 else (2 + dx, first)
                    row = 16 * (step % 4)
                    low, high = (panels[6 * side + which][at, row : row + 16, :].astype(F32) for side in (first_side, 1 - first_side))
                    rows = jnp.concatenate([low[:8], high[:8], low[8:], high[8:]], axis=0)
                    out_ref[group * 8 + (z ^ step)] = rows.astype(BF16)

    for side in range(2):
        pl.when(core == side)(functools.partial(fill, side))
    for group in range(8):
        slot, column = (group, 256 * group + 128) if group < 4 else (7 - group, 256 * (8 - group) + 128 * (2 * group - 8))
        out_ref[8 * slot : 8 * slot + 4, :, column : column + 128] = jnp.zeros((4, ROWS, 128), BF16)


def place_panels(place, panels):
    vmem = pl.BlockSpec(memory_space=pltpu.VMEM)
    return pl.pallas_call(
        place_kernel,
        in_specs=[pl.BlockSpec(memory_space=pltpu.SMEM)] + [vmem] * 12,
        out_specs=vmem,
        out_shape=jax.ShapeDtypeStruct((PEERS, ROWS, KEEP), BF16),
        compiler_params=pltpu.CompilerParams(vmem_limit_bytes=16 * 1024 * 1024),
    )(place, *panels)


def rotate_kernel(locked_ref, in_ref, matrix_ref, out_ref, held):
    low64 = lax.broadcasted_iota(jnp.int32, (64, 128), 0) % 8 < 4
    for group in range(8):
        rows = slice(256 * group, 256 * group + 256)
        for z in range(8):
            row = 256 * group + 32 * z
            for t in range(TILES):
                held[row : row + 32, 128 * t : 128 * t + 128] = in_ref[seat(z), group, 32 * t : 32 * t + 32, :]
        left = jnp.concatenate([in_ref[seat(z), group, 96:104, :] for z in range(8)], axis=0).astype(F32)
        parts = []
        for k in range(4):
            a = pltpu.roll(left, (-32 * k) % 128, 1)
            b = pltpu.roll(left, (-32 * k - 16) % 128, 1)
            parts.append(jnp.where(low64, a, b).reshape(8, 8, 128))
        held[rows, 384:512] = jnp.stack(parts, axis=1).reshape(256, 128).astype(BF16)

    def product(lhs, rhs):
        return lax.dot_general(lhs, rhs, (((0,), (0,)), ((), ())), preferred_element_type=F32)

    def panel(group, column, width, groups=1):
        return matrix_ref[8 * group : 8 * (group + groups), :, column : column + width].reshape(256 * groups, width)

    for block in range(8):
        total = None
        terms = []
        if block < 4:
            terms.append((panel(block, 256 * block, 256, 8 - block), held[256 * block :, :]))
        for peer in range(block, 8) if block >= 4 else ():
            at = 256 * (8 - peer) + 128 * (2 * block - 9)
            if block == 4:
                lhs = jnp.concatenate([panel(peer, 1024, 128), panel(7 - peer, at + 128, 128)], axis=1)
            else:
                lhs = panel(7 - peer, at, 256)
            terms.append((lhs, held[256 * peer : 256 * peer + 256, :]))
        for lhs, rhs in terms:
            term = product(lhs, rhs)
            total = term if total is None else total + term
        rows = lax.broadcasted_iota(jnp.int32, (256, 1), 0)
        limit = jnp.where(rows < 128, locked_ref[2 * block], locked_ref[2 * block + 1])
        mine = held[256 * block : 256 * block + 256, :].astype(F32)
        result = jnp.where(rows % 128 < limit, mine, total).astype(BF16)
        left = result[:, 384:512].astype(F32)
        for z in range(8):
            peer = place_of(8 * block + z)
            for t in range(TILES):
                out_ref[peer, 32 * t : 32 * t + 32, :] = result[32 * z : 32 * z + 32, 128 * t : 128 * t + 128]
            groups = regroup(left[32 * z : 32 * z + 32])
            out_ref[peer, 96:104, :] = gather_lanes(groups, 0).astype(BF16)


def rotate(locked, received, matrix):
    vmem = pl.BlockSpec(memory_space=pltpu.VMEM)
    return pl.pallas_call(
        rotate_kernel,
        in_specs=[pl.BlockSpec(memory_space=pltpu.SMEM), vmem, vmem],
        out_specs=vmem,
        out_shape=jax.ShapeDtypeStruct((PEERS, CHUNK, 128), BF16),
        scratch_shapes=[pltpu.VMEM((PEERS * ROWS, WIDTH), BF16)],
        compiler_params=pltpu.CompilerParams(vmem_limit_bytes=16 * 1024 * 1024),
    )(locked, received, matrix)


def exchange(value, axis, size, mask):
    return lax.ppermute(value, axis, [(i, i ^ mask) for i in range(size)])


def gather_near(rotation):
    rows = rotation[None]
    rows = jnp.concatenate([rows] + [exchange(rows, Z, 8, step) for step in (1, 2, 3)])
    late = [i for i in range(PEERS) if i >= 32]
    spare = rows[:, :, KEEP:]
    guests = [lax.ppermute(spare, EIG, [(i, (7 - i // 8) * 8 + (i % 8 ^ far)) for i in late]) for far in (0, 4)]
    return rows[:, :, :KEEP], exchange(rows[:, :, :KEEP], Z, 8, 4), *guests


def gather_panels(near, far, *guests):
    eig, yl = lax.axis_index(EIG), lax.axis_index("yl")
    group = eig // 8
    rows = jnp.concatenate([near, far])
    place = 256 * (group + 1)
    guest = jnp.concatenate([jnp.concatenate(guests), jnp.zeros((8, 8, KEEP), BF16)], axis=2)
    guest = lax.dynamic_update_slice(jnp.zeros((8, 8, 4096), BF16), guest, (0, 0, place))[:, :, :KEEP]
    cols = lax.broadcasted_iota(jnp.int32, (1, 1, KEEP), 2)
    rows = jnp.where((group >= 4) | (cols < place), rows, guest)
    other = exchange(rows, "yl", 2, 1)
    rows = jnp.where(yl == 0, jnp.stack([rows, other], axis=1), jnp.stack([other, rows], axis=1))

    a, b = rows[:4].reshape(1, 64, KEEP), rows[4:].reshape(1, 64, KEEP)
    b = jnp.concatenate([b, exchange(b, "yh", 2, 1)])
    a = jnp.concatenate([a] + [exchange(a, "x", 4, dx) for dx in (1, 2, 3)])
    far_a = exchange(a, "yh", 2, 1)
    far_b = [exchange(b, "x", 4, dx) for dx in (1, 2, 3)]
    a, b, far_a = lax.optimization_barrier((a, b, far_a))
    own = [a, far_a, b] + far_b
    return own + [exchange(panel, "c", 2, 1) for panel in own]


def body(vectors, rotation, locked):
    halfway = lax.all_to_all(pack(vectors), ("yh", "x"), split_axis=0, concat_axis=0, tiled=True)
    near = gather_near(rotation)
    halfway, _ = lax.optimization_barrier((halfway, near[1]))
    place = jnp.stack([lax.axis_index(name) for name in ("c", "yh", "x", Z)]).astype(jnp.int32)
    matrix = place_panels(place, gather_panels(*near))
    received = lax.all_to_all(halfway.transpose(1, 0, 2, 3), ("zl", "zh"), split_axis=0, concat_axis=0, tiled=True)
    back = lax.all_to_all(rotate(locked, received, matrix), ("x", "zl", "yh", "zh"), split_axis=0, concat_axis=0, tiled=True)
    return unpack(back)


def solution(mesh):
    fine = Mesh(mesh.devices.reshape(2, 4, 2, 4, 2, 2), AXES)
    in_specs = (P(EIG, SITE), P(EIG + SITE, None), P())
    return jax.shard_map(body, mesh=fine, in_specs=in_specs, out_specs=P(EIG, SITE), check_vma=False)
```

```python
import functools

import jax
import jax.numpy as jnp
from jax import lax
from jax.experimental import pallas as pl
from jax.experimental.pallas import tpu as pltpu
from jax.sharding import Mesh, PartitionSpec as P

AXES = ("yh", "x", "zh", "zl", "yl", "c")
Z = ("zh", "zl")
EIG = ("yh", "x", "zh", "zl")
SITE = ("yl", "c")
PEERS = 64
ROWS = 32
TILES = 3
CHUNK = 104
KEEP = 1152
WIDTH = 512
F32 = jnp.float32
BF16 = jnp.bfloat16


def seat(z):
    return z % 4 * 2 + z // 4


def place_of(peer):
    yh, x, z = peer // 32, peer // 8 % 4, peer % 8
    return ((x * 4 + z % 4) * 2 + yh) * 2 + z // 4


def lane_group():
    return lax.broadcasted_iota(jnp.int32, (8, 128), 1) // 16


def low_half():
    return lax.broadcasted_iota(jnp.int32, (8, 128), 0) < 4


def regroup(tile):
    low = low_half()
    groups = []
    for k in range(4):
        straight = tile[8 * k : 8 * k + 8]
        turned = pltpu.roll(straight, 4, 0)
        groups.append(jnp.where(low, straight, turned))
        groups.append(jnp.where(low, turned, straight))
    return groups


def gather_lanes(groups, place):
    lanes = lane_group()
    total = jnp.zeros((8, 128), F32)
    for h in range(8):
        total = jnp.where(lanes == h, pltpu.roll(groups[h], (16 * (h - place)) % 128, 1), total)
    return total


def pack_kernel(source_ref, target_ref, in_ref, out_ref, in_sems, out_sems):
    spans = [(24576, 1024)] + [(3072 * group, 3072) for group in range(8)]
    loads = []
    for index, (column, width) in enumerate(spans):
        columns = (slice(None), pl.ds(column, width))
        loads.append(pltpu.make_async_copy(source_ref.at[columns], in_ref.at[columns], in_sems.at[index]))
        loads[-1].start()
    loads[0].wait()
    stores = []
    for group in range(8):
        column = 24576 + 128 * group
        groups = regroup(in_ref[:, column : column + 128].astype(F32))
        for z in range(8):
            out_ref[group, seat(z), 96:104, :] = gather_lanes(groups, z).astype(BF16)
        loads[1 + group].wait()
        for z in range(8):
            for t in range(TILES):
                column = (TILES * (8 * group + z) + t) * 128
                out_ref[group, seat(z), 32 * t : 32 * t + 32, :] = in_ref[:, column : column + 128]
        stores.append(pltpu.make_async_copy(out_ref.at[group], target_ref.at[group], out_sems.at[group]))
        stores[-1].start()
    for store in stores:
        store.wait()


def pack(vectors):
    anywhere = pl.BlockSpec(memory_space=pl.ANY)
    return pl.pallas_call(
        pack_kernel,
        in_specs=[anywhere],
        out_specs=anywhere,
        out_shape=jax.ShapeDtypeStruct((8, 8, CHUNK, 128), BF16),
        scratch_shapes=[
            pltpu.VMEM((ROWS, 25600), BF16),
            pltpu.VMEM((8, 8, CHUNK, 128), BF16),
            pltpu.SemaphoreType.DMA((9,)),
            pltpu.SemaphoreType.DMA((8,)),
        ],
        compiler_params=pltpu.CompilerParams(vmem_limit_bytes=60 * 1024 * 1024),
    )(vectors)


def unpack_kernel(in_ref, target_ref, out_ref, sems):
    lanes, low = lane_group(), low_half()
    stores = []

    def store(column, width):
        columns = (slice(None), pl.ds(column, width))
        stores.append(pltpu.make_async_copy(out_ref.at[columns], target_ref.at[columns], sems.at[len(stores)]))
        stores[-1].start()

    for group in range(8):
        lefts = []
        for z in range(8):
            seat_of = place_of(8 * group + z)
            for t in range(TILES):
                column = (TILES * (8 * group + z) + t) * 128
                out_ref[:, column : column + 128] = in_ref[seat_of, 32 * t : 32 * t + 32, :]
            lefts.append(in_ref[seat_of, 96:104, :].astype(F32))
        store(3072 * group, 3072)
        pieces = []
        for k in range(4):
            total = jnp.zeros((8, 128), F32)
            for z in range(8):
                first = pltpu.roll(lefts[z], (16 * (z - 2 * k)) % 128, 1)
                second = pltpu.roll(lefts[z], (16 * (z - 2 * k - 1)) % 128, 1)
                total = jnp.where(lanes == z, jnp.where(low, first, second), total)
            pieces.append(total)
        column = 24576 + 128 * group
        out_ref[:, column : column + 128] = jnp.concatenate(pieces, axis=0).astype(BF16)
    store(24576, 1024)
    for copy in stores:
        copy.wait()


def unpack(received):
    return pl.pallas_call(
        unpack_kernel,
        in_specs=[pl.BlockSpec(memory_space=pltpu.VMEM)],
        out_specs=pl.BlockSpec(memory_space=pl.ANY),
        out_shape=jax.ShapeDtypeStruct((ROWS, 25600), BF16),
        scratch_shapes=[pltpu.VMEM((ROWS, 25600), BF16), pltpu.SemaphoreType.DMA((9,))],
        compiler_params=pltpu.CompilerParams(vmem_limit_bytes=16 * 1024 * 1024),
    )(received)


def place_kernel(place_ref, *refs):
    panels, (out_ref, matrix_ref, sems) = refs[:12], refs[12:]
    core, yh, x, z = (place_ref[i] for i in range(4))

    def copy(group, index):
        part = pl.ds(8 * group, 8)
        return pltpu.make_async_copy(matrix_ref.at[part], out_ref.at[part], sems.at[index])

    def fill(group, first, dx, first_side):
        for step in range(8):
            which, at = (first, dx) if step < 4 else (2 + dx, first)
            row = 16 * (step % 4)
            low, high = (panels[6 * side + which][at, row : row + 16, :].astype(F32) for side in (first_side, 1 - first_side))
            rows = jnp.concatenate([low[:8], high[:8], low[8:], high[8:]], axis=0)
            matrix_ref[group * 8 + (z ^ step)] = rows.astype(BF16)

    def mask(group):
        for column in (pl.multiple_of(256 * group + 128, 128), 1024):
            matrix_ref[pl.ds(8 * group, 4), :, pl.ds(column, 128)] = jnp.zeros((4, ROWS, 128), BF16)

    groups = [((yh ^ first) * 4 + (x ^ dx), first, dx) for first in range(2) for dx in range(4)]
    for index, (group, first, dx) in enumerate(groups):
        for side in range(2):
            pl.when(core == side)(functools.partial(fill, group, first, dx, side))
        pl.when(group < 4)(functools.partial(mask, group))
        copy(group, index).start()
    for index, (group, first, dx) in enumerate(groups):
        copy(group, index).wait()


def place_panels(place, panels):
    vmem = pl.BlockSpec(memory_space=pltpu.VMEM)
    return pl.pallas_call(
        place_kernel,
        in_specs=[pl.BlockSpec(memory_space=pltpu.SMEM)] + [vmem] * 12,
        out_specs=pl.BlockSpec(memory_space=pl.ANY),
        out_shape=jax.ShapeDtypeStruct((PEERS, ROWS, KEEP), BF16),
        scratch_shapes=[pltpu.VMEM((PEERS, ROWS, KEEP), BF16), pltpu.SemaphoreType.DMA((8,))],
        compiler_params=pltpu.CompilerParams(vmem_limit_bytes=50 * 1024 * 1024),
    )(place, *panels)


def rotate_kernel(locked_ref, in_ref, source_ref, out_ref, held, matrix_ref, sems):
    copies = []
    for group in range(8):
        part = pl.ds(8 * group, 8)
        copies.append(pltpu.make_async_copy(source_ref.at[part], matrix_ref.at[part], sems.at[group]))
        copies[-1].start()
    low64 = lax.broadcasted_iota(jnp.int32, (64, 128), 0) % 8 < 4
    for group in range(8):
        rows = slice(256 * group, 256 * group + 256)
        for z in range(8):
            row = 256 * group + 32 * z
            for t in range(TILES):
                held[row : row + 32, 128 * t : 128 * t + 128] = in_ref[seat(z), group, 32 * t : 32 * t + 32, :]
        left = jnp.concatenate([in_ref[seat(z), group, 96:104, :] for z in range(8)], axis=0).astype(F32)
        parts = []
        for k in range(4):
            a = pltpu.roll(left, (-32 * k) % 128, 1)
            b = pltpu.roll(left, (-32 * k - 16) % 128, 1)
            parts.append(jnp.where(low64, a, b).reshape(8, 8, 128))
        held[rows, 384:512] = jnp.stack(parts, axis=1).reshape(256, 128).astype(BF16)

    def product(lhs, rhs):
        return lax.dot_general(lhs, rhs, (((0,), (0,)), ((), ())), preferred_element_type=F32)

    def panel(group, column, width, groups=1):
        return matrix_ref[8 * group : 8 * (group + groups), :, column : column + width].reshape(256 * groups, width)

    for block in range(7, -1, -1):
        for copy in copies[7 - block : 8 - block] if block > 4 else copies[3:] if block == 4 else ():
            copy.wait()
        total = None
        terms = []
        if block < 4:
            terms.append((panel(block, 256 * block, 256, 8 - block), held[256 * block :, :]))
        for peer in range(block, 8) if block >= 4 else ():
            at = 256 * (8 - peer) + 128 * (2 * block - 9)
            if block == 4:
                lhs = jnp.concatenate([panel(peer, 1024, 128), panel(7 - peer, at + 128, 128)], axis=1)
            else:
                lhs = panel(7 - peer, at, 256)
            terms.append((lhs, held[256 * peer : 256 * peer + 256, :]))
        for lhs, rhs in terms:
            term = product(lhs, rhs)
            total = term if total is None else total + term
        rows = lax.broadcasted_iota(jnp.int32, (256, 1), 0)
        limit = jnp.where(rows < 128, locked_ref[2 * block], locked_ref[2 * block + 1])
        mine = held[256 * block : 256 * block + 256, :].astype(F32)
        result = jnp.where(rows % 128 < limit, mine, total).astype(BF16)
        left = result[:, 384:512].astype(F32)
        for z in range(8):
            peer = place_of(8 * block + z)
            for t in range(TILES):
                out_ref[peer, 32 * t : 32 * t + 32, :] = result[32 * z : 32 * z + 32, 128 * t : 128 * t + 128]
            groups = regroup(left[32 * z : 32 * z + 32])
            out_ref[peer, 96:104, :] = gather_lanes(groups, 0).astype(BF16)


def rotate(locked, received, matrix):
    vmem = pl.BlockSpec(memory_space=pltpu.VMEM)
    return pl.pallas_call(
        rotate_kernel,
        in_specs=[pl.BlockSpec(memory_space=pltpu.SMEM), vmem, pl.BlockSpec(memory_space=pl.ANY)],
        out_specs=vmem,
        out_shape=jax.ShapeDtypeStruct((PEERS, CHUNK, 128), BF16),
        scratch_shapes=[
            pltpu.VMEM((PEERS * ROWS, WIDTH), BF16),
            pltpu.VMEM((PEERS, ROWS, KEEP), BF16),
            pltpu.SemaphoreType.DMA((8,)),
        ],
        compiler_params=pltpu.CompilerParams(vmem_limit_bytes=50 * 1024 * 1024),
    )(locked, received, matrix)


def exchange(value, axis, size, mask):
    return lax.ppermute(value, axis, [(i, i ^ mask) for i in range(size)])


def gather_near(rotation):
    rows = rotation[None]
    rows = jnp.concatenate([rows] + [exchange(rows, Z, 8, step) for step in (1, 2, 3)])
    late = [i for i in range(PEERS) if i >= 32]
    spare = rows[:, :, KEEP:]
    guests = [lax.ppermute(spare, EIG, [(i, (7 - i // 8) * 8 + (i % 8 ^ far)) for i in late]) for far in (0, 4)]
    return rows[:, :, :KEEP], exchange(rows[:, :, :KEEP], Z, 8, 4), *guests


def gather_panels(near, far, *guests):
    eig, yl = lax.axis_index(EIG), lax.axis_index("yl")
    group = eig // 8
    rows = jnp.concatenate([near, far])
    place = 256 * (group + 1)
    guest = jnp.concatenate([jnp.concatenate(guests), jnp.zeros((8, 8, KEEP), BF16)], axis=2)
    guest = lax.dynamic_update_slice(jnp.zeros((8, 8, 4096), BF16), guest, (0, 0, place))[:, :, :KEEP]
    cols = lax.broadcasted_iota(jnp.int32, (1, 1, KEEP), 2)
    rows = jnp.where((group >= 4) | (cols < place), rows, guest)
    other = exchange(rows, "yl", 2, 1)
    rows = jnp.where(yl == 0, jnp.stack([rows, other], axis=1), jnp.stack([other, rows], axis=1))

    a, b = rows[:4].reshape(1, 64, KEEP), rows[4:].reshape(1, 64, KEEP)
    b = jnp.concatenate([b, exchange(b, "yh", 2, 1)])
    a = jnp.concatenate([a] + [exchange(a, "x", 4, dx) for dx in (1, 2, 3)])
    far_a = exchange(a, "yh", 2, 1)
    far_b = [exchange(b, "x", 4, dx) for dx in (1, 2, 3)]
    a, b, far_b[2] = lax.optimization_barrier((a, b, far_b[2]))
    own = [a, far_a, b] + far_b
    return own + [exchange(panel, "c", 2, 1) for panel in own]


def body(vectors, rotation, locked):
    halfway = lax.all_to_all(pack(vectors), ("yh", "x"), split_axis=0, concat_axis=0, tiled=True)
    near = gather_near(rotation)
    halfway, _ = lax.optimization_barrier((halfway, near[1]))
    place = jnp.stack([lax.axis_index(name) for name in ("c", "yh", "x", Z)]).astype(jnp.int32)
    matrix = place_panels(place, gather_panels(*near))
    received = lax.all_to_all(halfway.transpose(1, 0, 2, 3), ("zl", "zh"), split_axis=0, concat_axis=0, tiled=True)
    back = lax.all_to_all(rotate(locked, received, matrix), ("x", "zl", "yh", "zh"), split_axis=0, concat_axis=0, tiled=True)
    return unpack(back)


def solution(mesh):
    fine = Mesh(mesh.devices.reshape(2, 4, 2, 4, 2, 2), AXES)
    in_specs = (P(EIG, SITE), P(EIG + SITE, None), P())
    return jax.shard_map(body, mesh=fine, in_specs=in_specs, out_specs=P(EIG, SITE), check_vma=False)
```

```python
import functools

import jax
import jax.numpy as jnp
from jax import lax
from jax.experimental import pallas as pl
from jax.experimental.pallas import tpu as pltpu
from jax.sharding import Mesh, PartitionSpec as P

AXES = ("yh", "x", "zh", "zl", "yl", "c")
Z = ("zh", "zl")
EIG = ("yh", "x", "zh", "zl")
SITE = ("yl", "c")
PEERS = 64
ROWS = 32
TILES = 3
CHUNK = 104
KEEP = 1152
WIDTH = 512
F32 = jnp.float32
BF16 = jnp.bfloat16


def seat(z):
    return z % 4 * 2 + z // 4


def place_of(peer):
    yh, x, z = peer // 32, peer // 8 % 4, peer % 8
    return ((x * 4 + z % 4) * 2 + yh) * 2 + z // 4


def lane_group():
    return lax.broadcasted_iota(jnp.int32, (8, 128), 1) // 16


def low_half():
    return lax.broadcasted_iota(jnp.int32, (8, 128), 0) < 4


def regroup(tile):
    low = low_half()
    groups = []
    for k in range(4):
        straight = tile[8 * k : 8 * k + 8]
        turned = pltpu.roll(straight, 4, 0)
        groups.append(jnp.where(low, straight, turned))
        groups.append(jnp.where(low, turned, straight))
    return groups


def gather_lanes(groups, place):
    lanes = lane_group()
    total = jnp.zeros((8, 128), F32)
    for h in range(8):
        total = jnp.where(lanes == h, pltpu.roll(groups[h], (16 * (h - place)) % 128, 1), total)
    return total


def pack_kernel(source_ref, target_ref, in_ref, out_ref, in_sems, out_sems):
    spans = [(24576, 1024)] + [(3072 * group, 3072) for group in range(8)]
    loads = []
    for index, (column, width) in enumerate(spans):
        columns = (slice(None), pl.ds(column, width))
        loads.append(pltpu.make_async_copy(source_ref.at[columns], in_ref.at[columns], in_sems.at[index]))
        loads[-1].start()
    loads[0].wait()
    stores = []
    for group in range(8):
        column = 24576 + 128 * group
        groups = regroup(in_ref[:, column : column + 128].astype(F32))
        for z in range(8):
            out_ref[group, seat(z), 96:104, :] = gather_lanes(groups, z).astype(BF16)
        loads[1 + group].wait()
        for z in range(8):
            for t in range(TILES):
                column = (TILES * (8 * group + z) + t) * 128
                out_ref[group, seat(z), 32 * t : 32 * t + 32, :] = in_ref[:, column : column + 128]
        stores.append(pltpu.make_async_copy(out_ref.at[group], target_ref.at[group], out_sems.at[group]))
        stores[-1].start()
    for store in stores:
        store.wait()


def pack(vectors):
    anywhere = pl.BlockSpec(memory_space=pl.ANY)
    return pl.pallas_call(
        pack_kernel,
        in_specs=[anywhere],
        out_specs=anywhere,
        out_shape=jax.ShapeDtypeStruct((8, 8, CHUNK, 128), BF16),
        scratch_shapes=[
            pltpu.VMEM((ROWS, 25600), BF16),
            pltpu.VMEM((8, 8, CHUNK, 128), BF16),
            pltpu.SemaphoreType.DMA((9,)),
            pltpu.SemaphoreType.DMA((8,)),
        ],
        compiler_params=pltpu.CompilerParams(vmem_limit_bytes=60 * 1024 * 1024),
    )(vectors)


def unpack_kernel(in_ref, target_ref, out_ref, sems):
    lanes, low = lane_group(), low_half()
    stores = []

    def store(column, width):
        columns = (slice(None), pl.ds(column, width))
        stores.append(pltpu.make_async_copy(out_ref.at[columns], target_ref.at[columns], sems.at[len(stores)]))
        stores[-1].start()

    for group in range(8):
        lefts = []
        for z in range(8):
            seat_of = place_of(8 * group + z)
            for t in range(TILES):
                column = (TILES * (8 * group + z) + t) * 128
                out_ref[:, column : column + 128] = in_ref[seat_of, 32 * t : 32 * t + 32, :]
            lefts.append(in_ref[seat_of, 96:104, :].astype(F32))
        store(3072 * group, 3072)
        pieces = []
        for k in range(4):
            total = jnp.zeros((8, 128), F32)
            for z in range(8):
                first = pltpu.roll(lefts[z], (16 * (z - 2 * k)) % 128, 1)
                second = pltpu.roll(lefts[z], (16 * (z - 2 * k - 1)) % 128, 1)
                total = jnp.where(lanes == z, jnp.where(low, first, second), total)
            pieces.append(total)
        column = 24576 + 128 * group
        out_ref[:, column : column + 128] = jnp.concatenate(pieces, axis=0).astype(BF16)
    store(24576, 1024)
    for copy in stores:
        copy.wait()


def unpack(received):
    return pl.pallas_call(
        unpack_kernel,
        in_specs=[pl.BlockSpec(memory_space=pltpu.VMEM)],
        out_specs=pl.BlockSpec(memory_space=pl.ANY),
        out_shape=jax.ShapeDtypeStruct((ROWS, 25600), BF16),
        scratch_shapes=[pltpu.VMEM((ROWS, 25600), BF16), pltpu.SemaphoreType.DMA((9,))],
        compiler_params=pltpu.CompilerParams(vmem_limit_bytes=16 * 1024 * 1024),
    )(received)


def place_kernel(place_ref, *refs):
    panels, (out_ref, matrix_ref, sems) = refs[:12], refs[12:]
    core, yh, x, z = (place_ref[i] for i in range(4))

    def copy(group, index):
        part = pl.ds(8 * group, 8)
        return pltpu.make_async_copy(matrix_ref.at[part], out_ref.at[part], sems.at[index])

    def fill(group, first, dx, first_side):
        for step in range(8):
            which, at = (first, dx) if step < 4 else (2 + dx, first)
            row = 16 * (step % 4)
            low, high = (panels[6 * side + which][at, row : row + 16, :].astype(F32) for side in (first_side, 1 - first_side))
            rows = jnp.concatenate([low[:8], high[:8], low[8:], high[8:]], axis=0)
            matrix_ref[group * 8 + (z ^ step)] = rows.astype(BF16)

    def mask(group):
        for column in (pl.multiple_of(256 * group + 128, 128), 1024):
            matrix_ref[pl.ds(8 * group, 4), :, pl.ds(column, 128)] = jnp.zeros((4, ROWS, 128), BF16)

    groups = [((yh ^ first) * 4 + (x ^ dx), first, dx) for first in range(2) for dx in range(4)]
    for index, (group, first, dx) in enumerate(groups):
        for side in range(2):
            pl.when(core == side)(functools.partial(fill, group, first, dx, side))
        pl.when(group < 4)(functools.partial(mask, group))
        copy(group, index).start()
    for index, (group, first, dx) in enumerate(groups):
        copy(group, index).wait()


def place_panels(place, panels):
    vmem = pl.BlockSpec(memory_space=pltpu.VMEM)
    return pl.pallas_call(
        place_kernel,
        in_specs=[pl.BlockSpec(memory_space=pltpu.SMEM)] + [vmem] * 12,
        out_specs=pl.BlockSpec(memory_space=pl.ANY),
        out_shape=jax.ShapeDtypeStruct((PEERS, ROWS, KEEP), BF16),
        scratch_shapes=[pltpu.VMEM((PEERS, ROWS, KEEP), BF16), pltpu.SemaphoreType.DMA((8,))],
        compiler_params=pltpu.CompilerParams(vmem_limit_bytes=50 * 1024 * 1024),
    )(place, *panels)


def rotate_kernel(locked_ref, in_ref, source_ref, out_ref, held, matrix_ref, sems):
    copies = []
    for group in range(8):
        part = pl.ds(8 * group, 8)
        copies.append(pltpu.make_async_copy(source_ref.at[part], matrix_ref.at[part], sems.at[group]))
        copies[-1].start()
    low64 = lax.broadcasted_iota(jnp.int32, (64, 128), 0) % 8 < 4
    for group in range(8):
        rows = slice(256 * group, 256 * group + 256)
        for z in range(8):
            row = 256 * group + 32 * z
            for t in range(TILES):
                held[row : row + 32, 128 * t : 128 * t + 128] = in_ref[seat(z), group, 32 * t : 32 * t + 32, :]
        left = jnp.concatenate([in_ref[seat(z), group, 96:104, :] for z in range(8)], axis=0).astype(F32)
        parts = []
        for k in range(4):
            a = pltpu.roll(left, (-32 * k) % 128, 1)
            b = pltpu.roll(left, (-32 * k - 16) % 128, 1)
            parts.append(jnp.where(low64, a, b).reshape(8, 8, 128))
        held[rows, 384:512] = jnp.stack(parts, axis=1).reshape(256, 128).astype(BF16)

    def product(lhs, rhs):
        return lax.dot_general(lhs, rhs, (((0,), (0,)), ((), ())), preferred_element_type=F32)

    def panel(group, column, width, groups=1):
        return matrix_ref[8 * group : 8 * (group + groups), :, column : column + width].reshape(256 * groups, width)

    for block in range(7, -1, -1):
        for copy in copies[7 - block : 8 - block] if block > 4 else copies[3:] if block == 4 else ():
            copy.wait()
        total = None
        terms = []
        if block < 4:
            terms.append((panel(block, 256 * block, 256, 8 - block), held[256 * block :, :]))
        for peer in range(block, 8) if block >= 4 else ():
            at = 256 * (8 - peer) + 128 * (2 * block - 9)
            if block == 4:
                lhs = jnp.concatenate([panel(peer, 1024, 128), panel(7 - peer, at + 128, 128)], axis=1)
            else:
                lhs = panel(7 - peer, at, 256)
            terms.append((lhs, held[256 * peer : 256 * peer + 256, :]))
        for lhs, rhs in terms:
            term = product(lhs, rhs)
            total = term if total is None else total + term
        rows = lax.broadcasted_iota(jnp.int32, (256, 1), 0)
        limit = jnp.where(rows < 128, locked_ref[2 * block], locked_ref[2 * block + 1])
        mine = held[256 * block : 256 * block + 256, :].astype(F32)
        result = jnp.where(rows % 128 < limit, mine, total).astype(BF16)
        left = result[:, 384:512].astype(F32)
        for z in range(8):
            peer = place_of(8 * block + z)
            for t in range(TILES):
                out_ref[peer, 32 * t : 32 * t + 32, :] = result[32 * z : 32 * z + 32, 128 * t : 128 * t + 128]
            groups = regroup(left[32 * z : 32 * z + 32])
            out_ref[peer, 96:104, :] = gather_lanes(groups, 0).astype(BF16)


def rotate(locked, received, matrix):
    vmem = pl.BlockSpec(memory_space=pltpu.VMEM)
    return pl.pallas_call(
        rotate_kernel,
        in_specs=[pl.BlockSpec(memory_space=pltpu.SMEM), vmem, pl.BlockSpec(memory_space=pl.ANY)],
        out_specs=vmem,
        out_shape=jax.ShapeDtypeStruct((PEERS, CHUNK, 128), BF16),
        scratch_shapes=[
            pltpu.VMEM((PEERS * ROWS, WIDTH), BF16),
            pltpu.VMEM((PEERS, ROWS, KEEP), BF16),
            pltpu.SemaphoreType.DMA((8,)),
        ],
        compiler_params=pltpu.CompilerParams(vmem_limit_bytes=50 * 1024 * 1024),
    )(locked, received, matrix)


def exchange(value, axis, size, mask):
    return lax.ppermute(value, axis, [(i, i ^ mask) for i in range(size)])


def gather_near(rotation):
    rows = rotation[None]
    rows = jnp.concatenate([rows] + [exchange(rows, Z, 8, step) for step in (1, 2, 3)])
    late = [i for i in range(PEERS) if i >= 32]
    far = exchange(rows[:, :, :KEEP], Z, 8, 4)
    spare, far = lax.optimization_barrier((rows[:, :, KEEP:], far))
    guests = [lax.ppermute(spare, EIG, [(i, (7 - i // 8) * 8 + (i % 8 ^ half)) for i in late]) for half in (0, 4)]
    return rows[:, :, :KEEP], far, *guests


def gather_panels(near, far, *guests):
    eig, yl = lax.axis_index(EIG), lax.axis_index("yl")
    group = eig // 8
    rows = jnp.concatenate([near, far])
    place = 256 * (group + 1)
    guest = jnp.concatenate([jnp.concatenate(guests), jnp.zeros((8, 8, KEEP), BF16)], axis=2)
    guest = lax.dynamic_update_slice(jnp.zeros((8, 8, 4096), BF16), guest, (0, 0, place))[:, :, :KEEP]
    cols = lax.broadcasted_iota(jnp.int32, (1, 1, KEEP), 2)
    rows = jnp.where((group >= 4) | (cols < place), rows, guest)
    other = exchange(rows, "yl", 2, 1)
    rows = jnp.where(yl == 0, jnp.stack([rows, other], axis=1), jnp.stack([other, rows], axis=1))

    a, b = rows[:4].reshape(1, 64, KEEP), rows[4:].reshape(1, 64, KEEP)
    b = jnp.concatenate([b, exchange(b, "yh", 2, 1)])
    a = jnp.concatenate([a] + [exchange(a, "x", 4, dx) for dx in (1, 2, 3)])
    far_a = exchange(a, "yh", 2, 1)
    far_b = [exchange(b, "x", 4, dx) for dx in (1, 2, 3)]
    a, b, far_a = lax.optimization_barrier((a, b, far_a))
    own = [a, far_a, b] + far_b
    return own + [exchange(panel, "c", 2, 1) for panel in own]


def body(vectors, rotation, locked):
    halfway = lax.all_to_all(pack(vectors), ("yh", "x"), split_axis=0, concat_axis=0, tiled=True)
    near = gather_near(rotation)
    halfway, _ = lax.optimization_barrier((halfway, near[1]))
    place = jnp.stack([lax.axis_index(name) for name in ("c", "yh", "x", Z)]).astype(jnp.int32)
    matrix = place_panels(place, gather_panels(*near))
    received = lax.all_to_all(halfway.transpose(1, 0, 2, 3), ("zl", "zh"), split_axis=0, concat_axis=0, tiled=True)
    back = lax.all_to_all(rotate(locked, received, matrix), ("x", "zl", "yh", "zh"), split_axis=0, concat_axis=0, tiled=True)
    return unpack(back)


def solution(mesh):
    fine = Mesh(mesh.devices.reshape(2, 4, 2, 4, 2, 2), AXES)
    in_specs = (P(EIG, SITE), P(EIG + SITE, None), P())
    return jax.shard_map(body, mesh=fine, in_specs=in_specs, out_specs=P(EIG, SITE), check_vma=False)
```

```python
import functools

import jax
import jax.numpy as jnp
from jax import lax
from jax.experimental import pallas as pl
from jax.experimental.pallas import tpu as pltpu
from jax.sharding import Mesh, PartitionSpec as P

AXES = ("yh", "x", "zh", "zl", "yl", "c")
Z = ("zh", "zl")
EIG = ("yh", "x", "zh", "zl")
SITE = ("yl", "c")
PEERS = 64
ROWS = 32
TILES = 3
CHUNK = 104
KEEP = 1152
WIDTH = 512
F32 = jnp.float32
BF16 = jnp.bfloat16


def seat(z):
    return z % 4 * 2 + z // 4


def place_of(peer):
    yh, x, z = peer // 32, peer // 8 % 4, peer % 8
    return ((x * 4 + z % 4) * 2 + yh) * 2 + z // 4


def lane_group():
    return lax.broadcasted_iota(jnp.int32, (8, 128), 1) // 16


def low_half():
    return lax.broadcasted_iota(jnp.int32, (8, 128), 0) < 4


def regroup(tile):
    low = low_half()
    groups = []
    for k in range(4):
        straight = tile[8 * k : 8 * k + 8]
        turned = pltpu.roll(straight, 4, 0)
        groups.append(jnp.where(low, straight, turned))
        groups.append(jnp.where(low, turned, straight))
    return groups


def gather_lanes(groups, place):
    lanes = lane_group()
    total = jnp.zeros((8, 128), F32)
    for h in range(8):
        total = jnp.where(lanes == h, pltpu.roll(groups[h], (16 * (h - place)) % 128, 1), total)
    return total


def pack_kernel(source_ref, target_ref, in_ref, out_ref, in_sems, out_sems):
    spans = [(24576, 1024)] + [(3072 * group, 3072) for group in range(8)]
    loads = []
    for index, (column, width) in enumerate(spans):
        columns = (slice(None), pl.ds(column, width))
        loads.append(pltpu.make_async_copy(source_ref.at[columns], in_ref.at[columns], in_sems.at[index]))
        loads[-1].start()
    loads[0].wait()
    stores = []
    for group in range(8):
        column = 24576 + 128 * group
        groups = regroup(in_ref[:, column : column + 128].astype(F32))
        for z in range(8):
            out_ref[group, seat(z), 96:104, :] = gather_lanes(groups, z).astype(BF16)
        loads[1 + group].wait()
        for z in range(8):
            for t in range(TILES):
                column = (TILES * (8 * group + z) + t) * 128
                out_ref[group, seat(z), 32 * t : 32 * t + 32, :] = in_ref[:, column : column + 128]
        stores.append(pltpu.make_async_copy(out_ref.at[group], target_ref.at[group], out_sems.at[group]))
        stores[-1].start()
    for store in stores:
        store.wait()


def pack(vectors):
    anywhere = pl.BlockSpec(memory_space=pl.ANY)
    return pl.pallas_call(
        pack_kernel,
        in_specs=[anywhere],
        out_specs=anywhere,
        out_shape=jax.ShapeDtypeStruct((8, 8, CHUNK, 128), BF16),
        scratch_shapes=[
            pltpu.VMEM((ROWS, 25600), BF16),
            pltpu.VMEM((8, 8, CHUNK, 128), BF16),
            pltpu.SemaphoreType.DMA((9,)),
            pltpu.SemaphoreType.DMA((8,)),
        ],
        compiler_params=pltpu.CompilerParams(vmem_limit_bytes=60 * 1024 * 1024),
    )(vectors)


def unpack_kernel(in_ref, target_ref, out_ref, sems):
    lanes, low = lane_group(), low_half()
    stores = []

    def store(column, width):
        columns = (slice(None), pl.ds(column, width))
        stores.append(pltpu.make_async_copy(out_ref.at[columns], target_ref.at[columns], sems.at[len(stores)]))
        stores[-1].start()

    for group in range(8):
        lefts = []
        for z in range(8):
            seat_of = place_of(8 * group + z)
            for t in range(TILES):
                column = (TILES * (8 * group + z) + t) * 128
                out_ref[:, column : column + 128] = in_ref[seat_of, 32 * t : 32 * t + 32, :]
            lefts.append(in_ref[seat_of, 96:104, :].astype(F32))
        store(3072 * group, 3072)
        pieces = []
        for k in range(4):
            total = jnp.zeros((8, 128), F32)
            for z in range(8):
                first = pltpu.roll(lefts[z], (16 * (z - 2 * k)) % 128, 1)
                second = pltpu.roll(lefts[z], (16 * (z - 2 * k - 1)) % 128, 1)
                total = jnp.where(lanes == z, jnp.where(low, first, second), total)
            pieces.append(total)
        column = 24576 + 128 * group
        out_ref[:, column : column + 128] = jnp.concatenate(pieces, axis=0).astype(BF16)
    store(24576, 1024)
    for copy in stores:
        copy.wait()


def unpack(received):
    return pl.pallas_call(
        unpack_kernel,
        in_specs=[pl.BlockSpec(memory_space=pltpu.VMEM)],
        out_specs=pl.BlockSpec(memory_space=pl.ANY),
        out_shape=jax.ShapeDtypeStruct((ROWS, 25600), BF16),
        scratch_shapes=[pltpu.VMEM((ROWS, 25600), BF16), pltpu.SemaphoreType.DMA((9,))],
        compiler_params=pltpu.CompilerParams(vmem_limit_bytes=16 * 1024 * 1024),
    )(received)


def place_kernel(place_ref, *refs):
    panels, (out_ref, matrix_ref, sems) = refs[:12], refs[12:]
    core, yh, x, z = (place_ref[i] for i in range(4))

    def copy(group, index):
        part = pl.ds(8 * group, 8)
        return pltpu.make_async_copy(matrix_ref.at[part], out_ref.at[part], sems.at[index])

    def fill(group, first, dx, first_side):
        for step in range(8):
            which, at = (first, dx) if step < 4 else (2 + dx, first)
            row = 16 * (step % 4)
            low, high = (panels[6 * side + which][at, row : row + 16, :].astype(F32) for side in (first_side, 1 - first_side))
            rows = jnp.concatenate([low[:8], high[:8], low[8:], high[8:]], axis=0)
            matrix_ref[group * 8 + (z ^ step)] = rows.astype(BF16)

    def mask(group):
        for column in (pl.multiple_of(256 * group + 128, 128), 1024):
            matrix_ref[pl.ds(8 * group, 4), :, pl.ds(column, 128)] = jnp.zeros((4, ROWS, 128), BF16)

    groups = [((yh ^ first) * 4 + (x ^ dx), first, dx) for first in range(2) for dx in range(4)]
    for index, (group, first, dx) in enumerate(groups):
        for side in range(2):
            pl.when(core == side)(functools.partial(fill, group, first, dx, side))
        pl.when(group < 4)(functools.partial(mask, group))
        copy(group, index).start()
    for index, (group, first, dx) in enumerate(groups):
        copy(group, index).wait()


def place_panels(place, panels):
    vmem = pl.BlockSpec(memory_space=pltpu.VMEM)
    return pl.pallas_call(
        place_kernel,
        in_specs=[pl.BlockSpec(memory_space=pltpu.SMEM)] + [vmem] * 12,
        out_specs=pl.BlockSpec(memory_space=pl.ANY),
        out_shape=jax.ShapeDtypeStruct((PEERS, ROWS, KEEP), BF16),
        scratch_shapes=[pltpu.VMEM((PEERS, ROWS, KEEP), BF16), pltpu.SemaphoreType.DMA((8,))],
        compiler_params=pltpu.CompilerParams(vmem_limit_bytes=50 * 1024 * 1024),
    )(place, *panels)


def rotate_kernel(locked_ref, in_ref, source_ref, out_ref, held, matrix_ref, sems):
    copies = []
    for group in range(8):
        part = pl.ds(8 * group, 8)
        copies.append(pltpu.make_async_copy(source_ref.at[part], matrix_ref.at[part], sems.at[group]))
        copies[-1].start()
    low64 = lax.broadcasted_iota(jnp.int32, (64, 128), 0) % 8 < 4
    for group in range(8):
        rows = slice(256 * group, 256 * group + 256)
        for z in range(8):
            row = 256 * group + 32 * z
            for t in range(TILES):
                held[row : row + 32, 128 * t : 128 * t + 128] = in_ref[seat(z), group, 32 * t : 32 * t + 32, :]
        left = jnp.concatenate([in_ref[seat(z), group, 96:104, :] for z in range(8)], axis=0).astype(F32)
        parts = []
        for k in range(4):
            a = pltpu.roll(left, (-32 * k) % 128, 1)
            b = pltpu.roll(left, (-32 * k - 16) % 128, 1)
            parts.append(jnp.where(low64, a, b).reshape(8, 8, 128))
        held[rows, 384:512] = jnp.stack(parts, axis=1).reshape(256, 128).astype(BF16)

    def product(lhs, rhs):
        return lax.dot_general(lhs, rhs, (((0,), (0,)), ((), ())), preferred_element_type=F32)

    def panel(group, column, width, groups=1):
        return matrix_ref[8 * group : 8 * (group + groups), :, column : column + width].reshape(256 * groups, width)

    for block in range(7, -1, -1):
        for copy in copies[7 - block : 8 - block] if block > 4 else copies[3:] if block == 4 else ():
            copy.wait()
        total = None
        terms = []
        if block < 4:
            terms.append((panel(block, 256 * block, 256, 8 - block), held[256 * block :, :]))
        for peer in range(block, 8) if block >= 4 else ():
            at = 256 * (8 - peer) + 128 * (2 * block - 9)
            if block == 4:
                lhs = jnp.concatenate([panel(peer, 1024, 128), panel(7 - peer, at + 128, 128)], axis=1)
            else:
                lhs = panel(7 - peer, at, 256)
            terms.append((lhs, held[256 * peer : 256 * peer + 256, :]))
        for lhs, rhs in terms:
            term = product(lhs, rhs)
            total = term if total is None else total + term
        rows = lax.broadcasted_iota(jnp.int32, (256, 1), 0)
        limit = jnp.where(rows < 128, locked_ref[2 * block], locked_ref[2 * block + 1])
        mine = held[256 * block : 256 * block + 256, :].astype(F32)
        result = jnp.where(rows % 128 < limit, mine, total).astype(BF16)
        left = result[:, 384:512].astype(F32)
        for z in range(8):
            peer = place_of(8 * block + z)
            for t in range(TILES):
                out_ref[peer, 32 * t : 32 * t + 32, :] = result[32 * z : 32 * z + 32, 128 * t : 128 * t + 128]
            groups = regroup(left[32 * z : 32 * z + 32])
            out_ref[peer, 96:104, :] = gather_lanes(groups, 0).astype(BF16)


def rotate(locked, received, matrix):
    vmem = pl.BlockSpec(memory_space=pltpu.VMEM)
    return pl.pallas_call(
        rotate_kernel,
        in_specs=[pl.BlockSpec(memory_space=pltpu.SMEM), vmem, pl.BlockSpec(memory_space=pl.ANY)],
        out_specs=vmem,
        out_shape=jax.ShapeDtypeStruct((PEERS, CHUNK, 128), BF16),
        scratch_shapes=[
            pltpu.VMEM((PEERS * ROWS, WIDTH), BF16),
            pltpu.VMEM((PEERS, ROWS, KEEP), BF16),
            pltpu.SemaphoreType.DMA((8,)),
        ],
        compiler_params=pltpu.CompilerParams(vmem_limit_bytes=50 * 1024 * 1024),
    )(locked, received, matrix)


def exchange(value, axis, size, mask):
    return lax.ppermute(value, axis, [(i, i ^ mask) for i in range(size)])


def gather_near(rotation):
    rows = rotation[None]
    rows = jnp.concatenate([rows] + [exchange(rows, Z, 8, step) for step in (1, 2, 3)])
    parts = (rows[:, :, :KEEP], rows[:, :, KEEP:])
    return [jnp.concatenate([part, exchange(part, Z, 8, 4)]) for part in parts]


def gather_panels(keep, spare):
    eig, yl = lax.axis_index(EIG), lax.axis_index("yl")
    group = eig // 8
    late = [i for i in range(PEERS) if i >= 32]
    mirror = {i: (7 - i // 8) * 8 + i % 8 for i in late}
    keep, spare = lax.optimization_barrier((keep, spare))
    pairs = [[(2 * i + s, 2 * mirror[i] + (s ^ flip)) for i in late for s in range(2)] for flip in (0, 1)]
    guests = [lax.ppermute(spare, EIG + ("yl",), pair) for pair in pairs]
    other = exchange(keep, "yl", 2, 1)
    place = 256 * (group + 1)
    cols = lax.broadcasted_iota(jnp.int32, (1, 1, KEEP), 2)

    def fold(own, guest):
        guest = jnp.concatenate([guest, jnp.zeros((8, 8, KEEP), BF16)], axis=2)
        guest = lax.dynamic_update_slice(jnp.zeros((8, 8, 4096), BF16), guest, (0, 0, place))[:, :, :KEEP]
        return jnp.where((group >= 4) | (cols < place), own, guest)

    keep, other = fold(keep, guests[0]), fold(other, guests[1])
    rows = jnp.where(yl == 0, jnp.stack([keep, other], axis=1), jnp.stack([other, keep], axis=1))

    a, b = rows[:4].reshape(1, 64, KEEP), rows[4:].reshape(1, 64, KEEP)
    b = jnp.concatenate([b, exchange(b, "yh", 2, 1)])
    a = jnp.concatenate([a] + [exchange(a, "x", 4, dx) for dx in (1, 2, 3)])
    far_a = exchange(a, "yh", 2, 1)
    far_b = [exchange(b, "x", 4, dx) for dx in (1, 2, 3)]
    a, b, far_a = lax.optimization_barrier((a, b, far_a))
    own = [a, far_a, b] + far_b
    return own + [exchange(panel, "c", 2, 1) for panel in own]


def body(vectors, rotation, locked):
    halfway = lax.all_to_all(pack(vectors), ("yh", "x"), split_axis=0, concat_axis=0, tiled=True)
    keep, spare = gather_near(rotation)
    halfway, *_ = lax.optimization_barrier((halfway, keep, spare))
    place = jnp.stack([lax.axis_index(name) for name in ("c", "yh", "x", Z)]).astype(jnp.int32)
    matrix = place_panels(place, gather_panels(keep, spare))
    received = lax.all_to_all(halfway.transpose(1, 0, 2, 3), ("zl", "zh"), split_axis=0, concat_axis=0, tiled=True)
    back = lax.all_to_all(rotate(locked, received, matrix), ("x", "zl", "yh", "zh"), split_axis=0, concat_axis=0, tiled=True)
    return unpack(back)


def solution(mesh):
    fine = Mesh(mesh.devices.reshape(2, 4, 2, 4, 2, 2), AXES)
    in_specs = (P(EIG, SITE), P(EIG + SITE, None), P())
    return jax.shard_map(body, mesh=fine, in_specs=in_specs, out_specs=P(EIG, SITE), check_vma=False)
```

```python
import functools

import jax
import jax.numpy as jnp
from jax import lax
from jax.experimental import pallas as pl
from jax.experimental.pallas import tpu as pltpu
from jax.sharding import Mesh, PartitionSpec as P

AXES = ("yh", "x", "zh", "zl", "yl", "c")
Z = ("zh", "zl")
EIG = ("yh", "x", "zh", "zl")
SITE = ("yl", "c")
PEERS = 64
ROWS = 32
TILES = 3
CHUNK = 104
KEEP = 1152
WIDTH = 512
F32 = jnp.float32
BF16 = jnp.bfloat16


def seat(z):
    return z % 4 * 2 + z // 4


def place_of(peer):
    yh, x, z = peer // 32, peer // 8 % 4, peer % 8
    return ((x * 4 + z % 4) * 2 + yh) * 2 + z // 4


def lane_group():
    return lax.broadcasted_iota(jnp.int32, (8, 128), 1) // 16


def low_half():
    return lax.broadcasted_iota(jnp.int32, (8, 128), 0) < 4


def regroup(tile):
    low = low_half()
    groups = []
    for k in range(4):
        straight = tile[8 * k : 8 * k + 8]
        turned = pltpu.roll(straight, 4, 0)
        groups.append(jnp.where(low, straight, turned))
        groups.append(jnp.where(low, turned, straight))
    return groups


def gather_lanes(groups, place):
    lanes = lane_group()
    total = jnp.zeros((8, 128), F32)
    for h in range(8):
        total = jnp.where(lanes == h, pltpu.roll(groups[h], (16 * (h - place)) % 128, 1), total)
    return total


def pack_kernel(source_ref, target_ref, in_ref, out_ref, in_sems, out_sems):
    spans = [(24576, 1024)] + [(3072 * group, 3072) for group in range(8)]
    loads = []
    for index, (column, width) in enumerate(spans):
        columns = (slice(None), pl.ds(column, width))
        loads.append(pltpu.make_async_copy(source_ref.at[columns], in_ref.at[columns], in_sems.at[index]))
        loads[-1].start()
    loads[0].wait()
    stores = []
    for group in range(8):
        column = 24576 + 128 * group
        groups = regroup(in_ref[:, column : column + 128].astype(F32))
        for z in range(8):
            out_ref[group, seat(z), 96:104, :] = gather_lanes(groups, z).astype(BF16)
        loads[1 + group].wait()
        for z in range(8):
            for t in range(TILES):
                column = (TILES * (8 * group + z) + t) * 128
                out_ref[group, seat(z), 32 * t : 32 * t + 32, :] = in_ref[:, column : column + 128]
        stores.append(pltpu.make_async_copy(out_ref.at[group], target_ref.at[group], out_sems.at[group]))
        stores[-1].start()
    for store in stores:
        store.wait()


def pack(vectors):
    anywhere = pl.BlockSpec(memory_space=pl.ANY)
    return pl.pallas_call(
        pack_kernel,
        in_specs=[anywhere],
        out_specs=anywhere,
        out_shape=jax.ShapeDtypeStruct((8, 8, CHUNK, 128), BF16),
        scratch_shapes=[
            pltpu.VMEM((ROWS, 25600), BF16),
            pltpu.VMEM((8, 8, CHUNK, 128), BF16),
            pltpu.SemaphoreType.DMA((9,)),
            pltpu.SemaphoreType.DMA((8,)),
        ],
        compiler_params=pltpu.CompilerParams(vmem_limit_bytes=60 * 1024 * 1024),
    )(vectors)


def unpack_kernel(in_ref, target_ref, out_ref, sems):
    lanes, low = lane_group(), low_half()
    stores = []

    def store(column, width):
        columns = (slice(None), pl.ds(column, width))
        stores.append(pltpu.make_async_copy(out_ref.at[columns], target_ref.at[columns], sems.at[len(stores)]))
        stores[-1].start()

    for group in range(8):
        lefts = []
        for z in range(8):
            seat_of = place_of(8 * group + z)
            for t in range(TILES):
                column = (TILES * (8 * group + z) + t) * 128
                out_ref[:, column : column + 128] = in_ref[seat_of, 32 * t : 32 * t + 32, :]
            lefts.append(in_ref[seat_of, 96:104, :].astype(F32))
        store(3072 * group, 3072)
        pieces = []
        for k in range(4):
            total = jnp.zeros((8, 128), F32)
            for z in range(8):
                first = pltpu.roll(lefts[z], (16 * (z - 2 * k)) % 128, 1)
                second = pltpu.roll(lefts[z], (16 * (z - 2 * k - 1)) % 128, 1)
                total = jnp.where(lanes == z, jnp.where(low, first, second), total)
            pieces.append(total)
        column = 24576 + 128 * group
        out_ref[:, column : column + 128] = jnp.concatenate(pieces, axis=0).astype(BF16)
    store(24576, 1024)
    for copy in stores:
        copy.wait()


def unpack(received):
    return pl.pallas_call(
        unpack_kernel,
        in_specs=[pl.BlockSpec(memory_space=pltpu.VMEM)],
        out_specs=pl.BlockSpec(memory_space=pl.ANY),
        out_shape=jax.ShapeDtypeStruct((ROWS, 25600), BF16),
        scratch_shapes=[pltpu.VMEM((ROWS, 25600), BF16), pltpu.SemaphoreType.DMA((9,))],
        compiler_params=pltpu.CompilerParams(vmem_limit_bytes=16 * 1024 * 1024),
    )(received)


def place_kernel(place_ref, *refs):
    panels, (out_ref, matrix_ref, sems) = refs[:12], refs[12:]
    core, yh, x, z = (place_ref[i] for i in range(4))

    def copy(group, index):
        part = pl.ds(8 * group, 8)
        return pltpu.make_async_copy(matrix_ref.at[part], out_ref.at[part], sems.at[index])

    def fill(group, first, dx, first_side):
        for step in range(8):
            which, at = (first, dx) if step < 4 else (2 + dx, first)
            row = 16 * (step % 4)
            low, high = (panels[6 * side + which][at, row : row + 16, :].astype(F32) for side in (first_side, 1 - first_side))
            rows = jnp.concatenate([low[:8], high[:8], low[8:], high[8:]], axis=0)
            matrix_ref[group * 8 + (z ^ step)] = rows.astype(BF16)

    def mask(group):
        for column in (pl.multiple_of(256 * group + 128, 128), 1024):
            matrix_ref[pl.ds(8 * group, 4), :, pl.ds(column, 128)] = jnp.zeros((4, ROWS, 128), BF16)

    groups = [((yh ^ first) * 4 + (x ^ dx), first, dx) for first in range(2) for dx in range(4)]
    for index, (group, first, dx) in enumerate(groups):
        for side in range(2):
            pl.when(core == side)(functools.partial(fill, group, first, dx, side))
        pl.when(group < 4)(functools.partial(mask, group))
        copy(group, index).start()
    for index, (group, first, dx) in enumerate(groups):
        copy(group, index).wait()


def place_panels(place, panels):
    vmem = pl.BlockSpec(memory_space=pltpu.VMEM)
    return pl.pallas_call(
        place_kernel,
        in_specs=[pl.BlockSpec(memory_space=pltpu.SMEM)] + [vmem] * 12,
        out_specs=pl.BlockSpec(memory_space=pl.ANY),
        out_shape=jax.ShapeDtypeStruct((PEERS, ROWS, KEEP), BF16),
        scratch_shapes=[pltpu.VMEM((PEERS, ROWS, KEEP), BF16), pltpu.SemaphoreType.DMA((8,))],
        compiler_params=pltpu.CompilerParams(vmem_limit_bytes=50 * 1024 * 1024),
    )(place, *panels)


def rotate_kernel(locked_ref, in_ref, source_ref, out_ref, held, matrix_ref, sems):
    copies = []
    for group in range(8):
        part = pl.ds(8 * group, 8)
        copies.append(pltpu.make_async_copy(source_ref.at[part], matrix_ref.at[part], sems.at[group]))
        copies[-1].start()
    low64 = lax.broadcasted_iota(jnp.int32, (64, 128), 0) % 8 < 4
    for group in range(8):
        rows = slice(256 * group, 256 * group + 256)
        for z in range(8):
            row = 256 * group + 32 * z
            for t in range(TILES):
                held[row : row + 32, 128 * t : 128 * t + 128] = in_ref[seat(z), group, 32 * t : 32 * t + 32, :]
        left = jnp.concatenate([in_ref[seat(z), group, 96:104, :] for z in range(8)], axis=0).astype(F32)
        parts = []
        for k in range(4):
            a = pltpu.roll(left, (-32 * k) % 128, 1)
            b = pltpu.roll(left, (-32 * k - 16) % 128, 1)
            parts.append(jnp.where(low64, a, b).reshape(8, 8, 128))
        held[rows, 384:512] = jnp.stack(parts, axis=1).reshape(256, 128).astype(BF16)

    def product(lhs, rhs):
        return lax.dot_general(lhs, rhs, (((0,), (0,)), ((), ())), preferred_element_type=F32)

    def panel(group, column, width, groups=1):
        return matrix_ref[8 * group : 8 * (group + groups), :, column : column + width].reshape(256 * groups, width)

    for block in range(7, -1, -1):
        for copy in copies[7 - block : 8 - block] if block > 4 else copies[3:] if block == 4 else ():
            copy.wait()
        total = None
        terms = []
        if block < 4:
            terms.append((panel(block, 256 * block, 256, 8 - block), held[256 * block :, :]))
        for peer in range(block, 8) if block >= 4 else ():
            at = 256 * (8 - peer) + 128 * (2 * block - 9)
            if block == 4:
                lhs = jnp.concatenate([panel(peer, 1024, 128), panel(7 - peer, at + 128, 128)], axis=1)
            else:
                lhs = panel(7 - peer, at, 256)
            terms.append((lhs, held[256 * peer : 256 * peer + 256, :]))
        for lhs, rhs in terms:
            term = product(lhs, rhs)
            total = term if total is None else total + term
        rows = lax.broadcasted_iota(jnp.int32, (256, 1), 0)
        limit = jnp.where(rows < 128, locked_ref[2 * block], locked_ref[2 * block + 1])
        mine = held[256 * block : 256 * block + 256, :].astype(F32)
        result = jnp.where(rows % 128 < limit, mine, total).astype(BF16)
        left = result[:, 384:512].astype(F32)
        for z in range(8):
            peer = place_of(8 * block + z)
            for t in range(TILES):
                out_ref[peer, 32 * t : 32 * t + 32, :] = result[32 * z : 32 * z + 32, 128 * t : 128 * t + 128]
            groups = regroup(left[32 * z : 32 * z + 32])
            out_ref[peer, 96:104, :] = gather_lanes(groups, 0).astype(BF16)


def rotate(locked, received, matrix):
    vmem = pl.BlockSpec(memory_space=pltpu.VMEM)
    return pl.pallas_call(
        rotate_kernel,
        in_specs=[pl.BlockSpec(memory_space=pltpu.SMEM), vmem, pl.BlockSpec(memory_space=pl.ANY)],
        out_specs=vmem,
        out_shape=jax.ShapeDtypeStruct((PEERS, CHUNK, 128), BF16),
        scratch_shapes=[
            pltpu.VMEM((PEERS * ROWS, WIDTH), BF16),
            pltpu.VMEM((PEERS, ROWS, KEEP), BF16),
            pltpu.SemaphoreType.DMA((8,)),
        ],
        compiler_params=pltpu.CompilerParams(vmem_limit_bytes=50 * 1024 * 1024),
    )(locked, received, matrix)


def exchange(value, axis, size, mask):
    return lax.ppermute(value, axis, [(i, i ^ mask) for i in range(size)])


def gather_near(rotation):
    rows = rotation[None]
    rows = jnp.concatenate([rows] + [exchange(rows, Z, 8, step) for step in (1, 2, 3)])
    parts = (rows[:, :, :KEEP], rows[:, :, KEEP:])
    return [jnp.concatenate([part, exchange(part, Z, 8, 4)]) for part in parts]


def gather_panels(keep, spare, halfway):
    eig, yl = lax.axis_index(EIG), lax.axis_index("yl")
    group = eig // 8
    late = [i for i in range(PEERS) if i >= 32]
    mirror = {i: (7 - i // 8) * 8 + i % 8 for i in late}
    keep, spare = lax.optimization_barrier((keep, spare))
    pairs = [[(2 * i + s, 2 * mirror[i] + (s ^ flip)) for i in late for s in range(2)] for flip in (0, 1)]
    guests = [lax.ppermute(spare, EIG + ("yl",), pair) for pair in pairs]
    other = exchange(keep, "yl", 2, 1)
    *guests, _ = lax.optimization_barrier((*guests, halfway))
    place = 256 * (group + 1)
    cols = lax.broadcasted_iota(jnp.int32, (1, 1, KEEP), 2)

    def fold(own, guest):
        guest = jnp.concatenate([guest, jnp.zeros((8, 8, KEEP), BF16)], axis=2)
        guest = lax.dynamic_update_slice(jnp.zeros((8, 8, 4096), BF16), guest, (0, 0, place))[:, :, :KEEP]
        return jnp.where((group >= 4) | (cols < place), own, guest)

    keep, other = fold(keep, guests[0]), fold(other, guests[1])
    rows = jnp.where(yl == 0, jnp.stack([keep, other], axis=1), jnp.stack([other, keep], axis=1))

    a, b = rows[:4].reshape(1, 64, KEEP), rows[4:].reshape(1, 64, KEEP)
    b = jnp.concatenate([b, exchange(b, "yh", 2, 1)])
    a = jnp.concatenate([a] + [exchange(a, "x", 4, dx) for dx in (1, 2, 3)])
    far_a = exchange(a, "yh", 2, 1)
    far_b = [exchange(b, "x", 4, dx) for dx in (1, 2, 3)]
    a, b, far_a = lax.optimization_barrier((a, b, far_a))
    own = [a, far_a, b] + far_b
    return own + [exchange(panel, "c", 2, 1) for panel in own]


def body(vectors, rotation, locked):
    halfway = lax.all_to_all(pack(vectors), ("yh", "x"), split_axis=0, concat_axis=0, tiled=True)
    keep, spare = gather_near(rotation)
    halfway, *_ = lax.optimization_barrier((halfway, keep, spare))
    place = jnp.stack([lax.axis_index(name) for name in ("c", "yh", "x", Z)]).astype(jnp.int32)
    matrix = place_panels(place, gather_panels(keep, spare, halfway))
    received = lax.all_to_all(halfway.transpose(1, 0, 2, 3), ("zl", "zh"), split_axis=0, concat_axis=0, tiled=True)
    back = lax.all_to_all(rotate(locked, received, matrix), ("x", "zl", "yh", "zh"), split_axis=0, concat_axis=0, tiled=True)
    return unpack(back)


def solution(mesh):
    fine = Mesh(mesh.devices.reshape(2, 4, 2, 4, 2, 2), AXES)
    in_specs = (P(EIG, SITE), P(EIG + SITE, None), P())
    return jax.shard_map(body, mesh=fine, in_specs=in_specs, out_specs=P(EIG, SITE), check_vma=False)
```

```python
import functools

import jax
import jax.numpy as jnp
from jax import lax
from jax.experimental import pallas as pl
from jax.experimental.pallas import tpu as pltpu
from jax.sharding import Mesh, PartitionSpec as P

AXES = ("yh", "x", "zh", "zl", "yl", "c")
Z = ("zh", "zl")
EIG = ("yh", "x", "zh", "zl")
SITE = ("yl", "c")
PEERS = 64
ROWS = 32
TILES = 3
CHUNK = 104
KEEP = 1152
WIDTH = 512
F32 = jnp.float32
BF16 = jnp.bfloat16


def seat(z):
    return z % 4 * 2 + z // 4


def place_of(peer):
    yh, x, z = peer // 32, peer // 8 % 4, peer % 8
    return ((x * 4 + z % 4) * 2 + yh) * 2 + z // 4


def lane_group():
    return lax.broadcasted_iota(jnp.int32, (8, 128), 1) // 16


def low_half():
    return lax.broadcasted_iota(jnp.int32, (8, 128), 0) < 4


def regroup(tile):
    low = low_half()
    groups = []
    for k in range(4):
        straight = tile[8 * k : 8 * k + 8]
        turned = pltpu.roll(straight, 4, 0)
        groups.append(jnp.where(low, straight, turned))
        groups.append(jnp.where(low, turned, straight))
    return groups


def gather_lanes(groups, place):
    lanes = lane_group()
    total = jnp.zeros((8, 128), F32)
    for h in range(8):
        total = jnp.where(lanes == h, pltpu.roll(groups[h], (16 * (h - place)) % 128, 1), total)
    return total


def pack_kernel(source_ref, target_ref, in_ref, out_ref, in_sems, out_sems):
    spans = [(24576, 1024)] + [(3072 * group, 3072) for group in range(8)]
    loads = []
    for index, (column, width) in enumerate(spans):
        columns = (slice(None), pl.ds(column, width))
        loads.append(pltpu.make_async_copy(source_ref.at[columns], in_ref.at[columns], in_sems.at[index]))
        loads[-1].start()
    loads[0].wait()
    stores = []
    for group in range(8):
        column = 24576 + 128 * group
        groups = regroup(in_ref[:, column : column + 128].astype(F32))
        for z in range(8):
            out_ref[group, seat(z), 96:104, :] = gather_lanes(groups, z).astype(BF16)
        loads[1 + group].wait()
        for z in range(8):
            for t in range(TILES):
                column = (TILES * (8 * group + z) + t) * 128
                out_ref[group, seat(z), 32 * t : 32 * t + 32, :] = in_ref[:, column : column + 128]
        stores.append(pltpu.make_async_copy(out_ref.at[group], target_ref.at[group], out_sems.at[group]))
        stores[-1].start()
    for store in stores:
        store.wait()


def pack(vectors):
    anywhere = pl.BlockSpec(memory_space=pl.ANY)
    return pl.pallas_call(
        pack_kernel,
        in_specs=[anywhere],
        out_specs=anywhere,
        out_shape=jax.ShapeDtypeStruct((8, 8, CHUNK, 128), BF16),
        scratch_shapes=[
            pltpu.VMEM((ROWS, 25600), BF16),
            pltpu.VMEM((8, 8, CHUNK, 128), BF16),
            pltpu.SemaphoreType.DMA((9,)),
            pltpu.SemaphoreType.DMA((8,)),
        ],
        compiler_params=pltpu.CompilerParams(vmem_limit_bytes=60 * 1024 * 1024),
    )(vectors)


def unpack_kernel(in_ref, target_ref, out_ref, sems):
    lanes, low = lane_group(), low_half()
    stores = []

    def store(column, width):
        columns = (slice(None), pl.ds(column, width))
        stores.append(pltpu.make_async_copy(out_ref.at[columns], target_ref.at[columns], sems.at[len(stores)]))
        stores[-1].start()

    for group in range(8):
        lefts = []
        for z in range(8):
            seat_of = place_of(8 * group + z)
            for t in range(TILES):
                column = (TILES * (8 * group + z) + t) * 128
                out_ref[:, column : column + 128] = in_ref[seat_of, 32 * t : 32 * t + 32, :]
            lefts.append(in_ref[seat_of, 96:104, :].astype(F32))
        store(3072 * group, 3072)
        pieces = []
        for k in range(4):
            total = jnp.zeros((8, 128), F32)
            for z in range(8):
                first = pltpu.roll(lefts[z], (16 * (z - 2 * k)) % 128, 1)
                second = pltpu.roll(lefts[z], (16 * (z - 2 * k - 1)) % 128, 1)
                total = jnp.where(lanes == z, jnp.where(low, first, second), total)
            pieces.append(total)
        column = 24576 + 128 * group
        out_ref[:, column : column + 128] = jnp.concatenate(pieces, axis=0).astype(BF16)
    store(24576, 1024)
    for copy in stores:
        copy.wait()


def unpack(received):
    return pl.pallas_call(
        unpack_kernel,
        in_specs=[pl.BlockSpec(memory_space=pltpu.VMEM)],
        out_specs=pl.BlockSpec(memory_space=pl.ANY),
        out_shape=jax.ShapeDtypeStruct((ROWS, 25600), BF16),
        scratch_shapes=[pltpu.VMEM((ROWS, 25600), BF16), pltpu.SemaphoreType.DMA((9,))],
        compiler_params=pltpu.CompilerParams(vmem_limit_bytes=16 * 1024 * 1024),
    )(received)


def place_kernel(place_ref, *refs):
    panels, (out_ref, matrix_ref, sems) = refs[:12], refs[12:]
    core, yh, x, z = (place_ref[i] for i in range(4))

    def copy(group, index):
        part = pl.ds(8 * group, 8)
        return pltpu.make_async_copy(matrix_ref.at[part], out_ref.at[part], sems.at[index])

    def fill(group, first, dx, first_side):
        for step in range(8):
            which, at = (first, dx) if step < 4 else (2 + dx, first)
            row = 16 * (step % 4)
            low, high = (panels[6 * side + which][at, row : row + 16, :].astype(F32) for side in (first_side, 1 - first_side))
            rows = jnp.concatenate([low[:8], high[:8], low[8:], high[8:]], axis=0)
            matrix_ref[group * 8 + (z ^ step)] = rows.astype(BF16)

    def mask(group):
        for column in (pl.multiple_of(256 * group + 128, 128), 1024):
            matrix_ref[pl.ds(8 * group, 4), :, pl.ds(column, 128)] = jnp.zeros((4, ROWS, 128), BF16)

    groups = [((yh ^ first) * 4 + (x ^ dx), first, dx) for first in range(2) for dx in range(4)]
    for index, (group, first, dx) in enumerate(groups):
        for side in range(2):
            pl.when(core == side)(functools.partial(fill, group, first, dx, side))
        pl.when(group < 4)(functools.partial(mask, group))
        copy(group, index).start()
    for index, (group, first, dx) in enumerate(groups):
        copy(group, index).wait()


def place_panels(place, panels):
    vmem = pl.BlockSpec(memory_space=pltpu.VMEM)
    return pl.pallas_call(
        place_kernel,
        in_specs=[pl.BlockSpec(memory_space=pltpu.SMEM)] + [vmem] * 12,
        out_specs=pl.BlockSpec(memory_space=pl.ANY),
        out_shape=jax.ShapeDtypeStruct((PEERS, ROWS, KEEP), BF16),
        scratch_shapes=[pltpu.VMEM((PEERS, ROWS, KEEP), BF16), pltpu.SemaphoreType.DMA((8,))],
        compiler_params=pltpu.CompilerParams(vmem_limit_bytes=50 * 1024 * 1024),
    )(place, *panels)


def rotate_kernel(locked_ref, in_ref, source_ref, out_ref, held, matrix_ref, sems):
    copies = []
    for group in range(8):
        part = pl.ds(8 * group, 8)
        copies.append(pltpu.make_async_copy(source_ref.at[part], matrix_ref.at[part], sems.at[group]))
        copies[-1].start()
    low64 = lax.broadcasted_iota(jnp.int32, (64, 128), 0) % 8 < 4
    for group in range(8):
        rows = slice(256 * group, 256 * group + 256)
        for z in range(8):
            row = 256 * group + 32 * z
            for t in range(TILES):
                held[row : row + 32, 128 * t : 128 * t + 128] = in_ref[seat(z), group, 32 * t : 32 * t + 32, :]
        left = jnp.concatenate([in_ref[seat(z), group, 96:104, :] for z in range(8)], axis=0).astype(F32)
        parts = []
        for k in range(4):
            a = pltpu.roll(left, (-32 * k) % 128, 1)
            b = pltpu.roll(left, (-32 * k - 16) % 128, 1)
            parts.append(jnp.where(low64, a, b).reshape(8, 8, 128))
        held[rows, 384:512] = jnp.stack(parts, axis=1).reshape(256, 128).astype(BF16)

    def product(lhs, rhs):
        return lax.dot_general(lhs, rhs, (((0,), (0,)), ((), ())), preferred_element_type=F32)

    def panel(group, column, width, groups=1):
        return matrix_ref[8 * group : 8 * (group + groups), :, column : column + width].reshape(256 * groups, width)

    for block in range(7, -1, -1):
        for copy in copies[7 - block : 8 - block] if block > 4 else copies[3:] if block == 4 else ():
            copy.wait()
        total = None
        terms = []
        if block < 4:
            terms.append((panel(block, 256 * block, 256, 8 - block), held[256 * block :, :]))
        for peer in range(block, 8) if block >= 4 else ():
            at = 256 * (8 - peer) + 128 * (2 * block - 9)
            if block == 4:
                lhs = jnp.concatenate([panel(peer, 1024, 128), panel(7 - peer, at + 128, 128)], axis=1)
            else:
                lhs = panel(7 - peer, at, 256)
            terms.append((lhs, held[256 * peer : 256 * peer + 256, :]))
        for lhs, rhs in terms:
            term = product(lhs, rhs)
            total = term if total is None else total + term
        rows = lax.broadcasted_iota(jnp.int32, (256, 1), 0)
        limit = jnp.where(rows < 128, locked_ref[2 * block], locked_ref[2 * block + 1])
        mine = held[256 * block : 256 * block + 256, :].astype(F32)
        result = jnp.where(rows % 128 < limit, mine, total).astype(BF16)
        left = result[:, 384:512].astype(F32)
        for z in range(8):
            peer = place_of(8 * block + z)
            for t in range(TILES):
                out_ref[peer, 32 * t : 32 * t + 32, :] = result[32 * z : 32 * z + 32, 128 * t : 128 * t + 128]
            groups = regroup(left[32 * z : 32 * z + 32])
            out_ref[peer, 96:104, :] = gather_lanes(groups, 0).astype(BF16)


def rotate(locked, received, matrix):
    vmem = pl.BlockSpec(memory_space=pltpu.VMEM)
    return pl.pallas_call(
        rotate_kernel,
        in_specs=[pl.BlockSpec(memory_space=pltpu.SMEM), vmem, pl.BlockSpec(memory_space=pl.ANY)],
        out_specs=vmem,
        out_shape=jax.ShapeDtypeStruct((PEERS, CHUNK, 128), BF16),
        scratch_shapes=[
            pltpu.VMEM((PEERS * ROWS, WIDTH), BF16),
            pltpu.VMEM((PEERS, ROWS, KEEP), BF16),
            pltpu.SemaphoreType.DMA((8,)),
        ],
        compiler_params=pltpu.CompilerParams(vmem_limit_bytes=50 * 1024 * 1024),
    )(locked, received, matrix)


def exchange(value, axis, size, mask):
    return lax.ppermute(value, axis, [(i, i ^ mask) for i in range(size)])


def gather_near(rotation):
    rows = rotation[None]
    rows = jnp.concatenate([rows] + [exchange(rows, Z, 8, step) for step in (1, 2, 3)])
    parts = (rows[:, :, :KEEP], rows[:, :, KEEP:])
    return [jnp.concatenate([part, exchange(part, Z, 8, 4)]) for part in parts]


def gather_panels(keep, spare, halfway):
    eig, yl = lax.axis_index(EIG), lax.axis_index("yl")
    group = eig // 8
    late = [i for i in range(PEERS) if i >= 32]
    mirror = {i: (7 - i // 8) * 8 + i % 8 for i in late}
    keep, spare = lax.optimization_barrier((keep, spare))
    pairs = [[(2 * i + s, 2 * mirror[i] + (s ^ flip)) for i in late for s in range(2)] for flip in (0, 1)]
    guests = [lax.ppermute(spare, EIG + ("yl",), pair) for pair in pairs]
    other = exchange(keep, "yl", 2, 1)
    *guests, _ = lax.optimization_barrier((*guests, halfway))
    place = 256 * (group + 1)
    cols = lax.broadcasted_iota(jnp.int32, (1, 1, KEEP), 2)

    def fold(own, guest):
        guest = jnp.concatenate([guest, jnp.zeros((8, 8, KEEP), BF16)], axis=2)
        guest = lax.dynamic_update_slice(jnp.zeros((8, 8, 4096), BF16), guest, (0, 0, place))[:, :, :KEEP]
        return jnp.where((group >= 4) | (cols < place), own, guest)

    keep, other = fold(keep, guests[0]), fold(other, guests[1])
    rows = jnp.where(yl == 0, jnp.stack([keep, other], axis=1), jnp.stack([other, keep], axis=1))

    a, b = rows[:4].reshape(1, 64, KEEP), rows[4:].reshape(1, 64, KEEP)
    b = jnp.concatenate([b, exchange(b, "yh", 2, 1)])
    a = jnp.concatenate([a] + [exchange(a, "x", 4, dx) for dx in (1, 2, 3)])
    far_a = exchange(a, "yh", 2, 1)
    far_b = [exchange(b, "x", 4, dx) for dx in (1, 2, 3)]
    a, b, far_b[2] = lax.optimization_barrier((a, b, far_b[2]))
    own = [a, far_a, b] + far_b
    return own + [exchange(panel, "c", 2, 1) for panel in own]


def body(vectors, rotation, locked):
    halfway = lax.all_to_all(pack(vectors), ("yh", "x"), split_axis=0, concat_axis=0, tiled=True)
    keep, spare = gather_near(rotation)
    halfway, *_ = lax.optimization_barrier((halfway, keep, spare))
    place = jnp.stack([lax.axis_index(name) for name in ("c", "yh", "x", Z)]).astype(jnp.int32)
    matrix = place_panels(place, gather_panels(keep, spare, halfway))
    received = lax.all_to_all(halfway.transpose(1, 0, 2, 3), ("zl", "zh"), split_axis=0, concat_axis=0, tiled=True)
    back = lax.all_to_all(rotate(locked, received, matrix), ("x", "zl", "yh", "zh"), split_axis=0, concat_axis=0, tiled=True)
    return unpack(back)


def solution(mesh):
    fine = Mesh(mesh.devices.reshape(2, 4, 2, 4, 2, 2), AXES)
    in_specs = (P(EIG, SITE), P(EIG + SITE, None), P())
    return jax.shard_map(body, mesh=fine, in_specs=in_specs, out_specs=P(EIG, SITE), check_vma=False)
```
